256 devices in a mesh: seq: 32 (over y, z_lo, core), ch: 8 (over z_hi, x).
Axes of the slice: x: 4, y: 4, z: 8 (z_hi: 2, z_lo: 4; z = z_hi * 4 + z_lo), core: 2. Of those that a mesh axis runs over, the one named last changes fastest.
Arguments:
- gate_out: bfloat16 [8192, 4096], P('seq', 'ch'), may hold values from -6 to 6
- gate_in: bfloat16 [8192, 4096], P('seq', 'ch'), may hold values from -6 to 6
- values: bfloat16 [8192, 4096], P('seq', 'ch'), may hold values from -6 to 6
- grad_out: bfloat16 [8192, 8192], P('seq', 'ch'), may hold values from -6 to 6
- w_out: bfloat16 [4096, 8192], P('ch'), may hold values from -0.0625 to 0.0625
- filter_raw: bfloat16 [8192, 4096], P('seq', 'ch'), may hold values from -6 to 6
- skip: float32 [4096], P('ch'), may hold values from -1 to 1
Outputs:
- grad_gate_out: bfloat16 [8192, 4096], P('seq', 'ch')
- grad_gate_in: bfloat16 [8192, 4096], P('seq', 'ch')
- grad_values: bfloat16 [8192, 4096], P('seq', 'ch')
- grad_filter: bfloat16 [8192, 4096], P('seq', 'ch')
- grad_skip: bfloat16 [4096], P('ch')
The draws below stay inside these ranges and needn't reach their ends.
All inputs are finite; a program needn't handle non-finite values.
Results may differ from the reference program's by a relative error of at most 0.014.
Values may be sent and summed in bfloat16 or wider, within the bound.
A program may use at most 128 MiB of HBM per device.

```python
import jax
import jax.numpy as jnp
from jax import lax

D = 8192
CH = 4096
SEQ = 8192


def block_levels(stream_key, shape, cuts, smallest, largest):
    loudness = 1.0
    for dim, blocks in cuts:
        heights = jax.random.uniform(jax.random.fold_in(jax.random.fold_in(stream_key, 6), dim), (blocks,), jnp.float32, smallest / len(cuts), largest / len(cuts))
        loudness = loudness * jnp.repeat(jnp.exp(heights), shape[dim] // blocks).reshape((-1,) + (1,) * (len(shape) - 1 - dim))
    return loudness


def centred(stream_key, shape, width, bound, shards=(), kind=jnp.bfloat16):
    result = jax.random.normal(stream_key, shape, jnp.float32) * width
    if len(shards) > 0:
        result = block_levels(stream_key, shape, shards, -0.22, 0.18) * result
    return jnp.clip(result, min=-bound, max=bound).astype(kind)


def setup_inputs(seed: int = 0) -> dict:
    arg_keys = jax.random.split(jax.random.key(seed), 8)
    return {
        "gate_out": centred(arg_keys[0], (SEQ, CH), 1.0, 6.0, ((0, 32), (1, 8))),
        "gate_in": centred(arg_keys[1], (SEQ, CH), 1.0, 6.0, ((0, 32), (1, 8))),
        "values": centred(arg_keys[2], (SEQ, CH), 1.0, 6.0, ((0, 32), (1, 8))),
        "grad_out": centred(arg_keys[3], (SEQ, D), 1.0, 6.0, ((0, 32), (1, 8))),
        "w_out": centred(arg_keys[4], (CH, D), D ** -0.5, 0.0625, ((0, 8),)),
        "filter_raw": centred(arg_keys[5], (SEQ, CH), 1.0, 6.0, ((0, 32), (1, 8))),
        "skip": jnp.clip(jax.random.uniform(arg_keys[6], (CH,), jnp.float32, -1.0, 1.0) * block_levels(arg_keys[6], (CH,), ((0, 8),), -0.4, 0.0), -1.0, 1.0),
    }


def channel_block(packed):
    gate_out, gate_in, values, grad_z, filter_raw, skip = packed
    taps = filter_raw.astype(jnp.float32) / SEQ ** 0.5
    gated = (gate_in.astype(jnp.float32) * values.astype(jnp.float32)).astype(jnp.bfloat16)
    grad_y = (grad_z * gate_out.astype(jnp.float32)).astype(jnp.bfloat16)
    length = 2 * SEQ
    spec_g = jnp.fft.rfft(gated.astype(jnp.float32), length, axis=0)
    spec_d = jnp.fft.rfft(grad_y.astype(jnp.float32), length, axis=0)
    spec_f = jnp.fft.rfft(taps, length, axis=0)
    conv_out = jnp.fft.irfft(spec_f * spec_g, length, axis=0)[:SEQ]
    conv_back = jnp.fft.irfft(jnp.conj(spec_f) * spec_d, length, axis=0)[:SEQ]
    filter_grad = jnp.fft.irfft(jnp.conj(spec_g) * spec_d, length, axis=0)[:SEQ]
    gated_f = gated.astype(jnp.float32)
    grad_yf = grad_y.astype(jnp.float32)
    grad_gate_out = (grad_z * (conv_out + skip[None, :] * gated_f)).astype(jnp.bfloat16)
    grad_mixed = conv_back + skip[None, :] * grad_yf
    grad_gate_in = (grad_mixed * values.astype(jnp.float32)).astype(jnp.bfloat16)
    grad_values = (grad_mixed * gate_in.astype(jnp.float32)).astype(jnp.bfloat16)
    grad_filter = (filter_grad / SEQ ** 0.5).astype(jnp.bfloat16)
    grad_skip = (jnp.sum(grad_yf * gated_f, axis=0) / SEQ).astype(jnp.bfloat16)
    return grad_gate_out, grad_gate_in, grad_values, grad_filter, grad_skip


def reference(gate_out, gate_in, values, grad_out, w_out, filter_raw, skip):
    grad_z = jnp.dot(grad_out, w_out.T, preferred_element_type=jnp.float32)
    lane_width = 128
    pieces = CH // lane_width

    def split_cols(array):
        return array.reshape(array.shape[0], pieces, lane_width).transpose(1, 0, 2)

    def join_cols(array):
        return array.transpose(1, 0, 2).reshape(array.shape[1], CH)

    packed = (split_cols(gate_out), split_cols(gate_in), split_cols(values), split_cols(grad_z),
              split_cols(filter_raw), skip.reshape(pieces, lane_width))
    results = lax.map(channel_block, packed)
    return (join_cols(results[0]), join_cols(results[1]), join_cols(results[2]),
            join_cols(results[3]), results[4].reshape(CH))
```

```python
import functools
import math

import jax
import jax.numpy as jnp
import ml_dtypes
import numpy as np
from jax import lax
from jax.experimental import pallas as pl
from jax.experimental.pallas import tpu as pltpu
from jax.sharding import PartitionSpec as P

MESH = pl.DeviceIdType.MESH
bf16, f32 = jnp.bfloat16, jnp.float32

SEQ_DEVS = 32
CH_DEVS = 8
BLOCK = 256
CHANS = 512
OWN = CHANS // SEQ_DEVS
TOTAL = SEQ_DEVS * BLOCK
WIDTH = 1024
CHUNKS = 4
CW = WIDTH // CHUNKS
ROWS = 256
SCALE = 1.0 / (TOTAL * math.sqrt(TOTAL))


def tables():
    j = np.arange(SEQ_DEVS)
    ang = 2 * np.pi * (j[:, None] + 0.25) * j[None, :] / SEQ_DEVS
    eye = np.eye(OWN)
    parts = []
    for part in (np.cos(ang), -np.sin(ang)):
        parts.append(np.einsum("jp,ab->ajpb", part, eye).reshape(CHANS, CHANS))
    first = np.concatenate(parts, 0)
    m = np.arange(BLOCK)
    ang = 2 * np.pi * ((m[:, None] * m[None, :]) % BLOCK) / BLOCK
    cos, sin = np.cos(ang), np.sin(ang)
    second = np.block([[cos, -sin], [sin, cos]])
    ang = 2 * np.pi * (j[:, None] + 0.25) * m[None, :] / TOTAL
    turn = np.stack([np.cos(ang), -np.sin(ang)])
    cast = lambda a: a.astype(np.float32).astype(ml_dtypes.bfloat16)
    return cast(first), cast(first.T), cast(second), turn.astype(np.float32)


def nt(a, b):
    return lax.dot_general(a, b, (((1,), (1,)), ((), ())), preferred_element_type=f32)


def kernel(
    gate_out_hbm, gate_in_hbm, values_hbm, grad_out_hbm, w_hbm, filt_hbm, skip_ref, first_hbm, last_hbm, second_hbm, turn_ref,
    ggo_ref, ggi_ref, gv_ref, gf_ref, gs_ref,
    G, W, first, last, second, gate_out, gate_in, values, filt,
    goT, SB, XB, OB, RB, KS, RS, acc, gz, Y, Zs,
    lsem, gsem, sx, rx, sf, rf, sz, rz, sa, ra, so, ro, sk, rk,
):
    s, c = lax.axis_index("seq"), lax.axis_index("ch")
    zbase = (c // 4) * 4
    x = lax.rem(c, 4)
    right, left, far = (s, zbase + lax.rem(x + 1, 4)), (s, zbase + lax.rem(x + 3, 4)), (s, lax.rem(c + 4, 8))

    def block(q, step):
        base = zbase if q == 0 else 4 - zbase
        return base + lax.rem(x + step + 4, 4)

    loads = [(gate_in_hbm, gate_in), (values_hbm, values), (filt_hbm, filt), (gate_out_hbm, gate_out), (w_hbm, W),
             (first_hbm, first), (second_hbm, second), (last_hbm, last)]
    own = [pltpu.make_async_copy(grad_out_hbm.at[:, pl.ds(k * CW, CW)], G.at[c, k], gsem.at[k]) for k in range(CHUNKS)]
    for cp in own:
        cp.start()
    loads = [pltpu.make_async_copy(a, b, lsem.at[i]) for i, (a, b) in enumerate(loads)]
    for cp in loads:
        cp.start()

    barrier = pltpu.get_barrier_semaphore()
    for dev in (right, left, far):
        pl.semaphore_signal(barrier, inc=1, device_id=dev, device_id_type=MESH)

    def greet(i, _):
        pl.semaphore_signal(barrier, inc=1, device_id=(lax.rem(s + i, SEQ_DEVS), c), device_id_type=MESH)
        return 0

    lax.fori_loop(1, SEQ_DEVS, greet, 0)
    pl.semaphore_wait(barrier, SEQ_DEVS + 2)

    def remote(src, dst, ssem, rsem, dev):
        return pltpu.make_async_remote_copy(
            src_ref=src, dst_ref=dst, send_sem=ssem, recv_sem=rsem, device_id=dev, device_id_type=MESH
        )

    def xcopy(q, d, k, step=0):
        ref = G.at[block(q, step), k]
        return remote(ref, ref, sx.at[q, d, k], rx.at[q, d, k], (right, left)[d])

    def fcopy(q, d, k, step):
        ref = G.at[block(q, step), k]
        return remote(ref, ref, sf.at[q, d, k // 2], rf.at[q, d, k // 2], (right, left)[d])

    def zcopy(k, q=0):
        ref = G.at[block(q, 0), k]
        return remote(ref, ref, sz.at[k], rz.at[k], far)

    def spread_start(buf, dst, ssem, rsem, tail=()):
        def one(i, _):
            d = lax.rem(s + i, SEQ_DEVS)
            remote(buf.at[d], dst.at[s], ssem, rsem, (d, c)).start()
            return 0

        lax.fori_loop(1, SEQ_DEVS, one, 0)

    def spread_wait(buf, sem):
        part = buf.at[pl.ds(0, SEQ_DEVS - 1)]
        pltpu.make_async_copy(part, part, sem).wait()

    for k in range(CHUNKS):
        own[k].wait()
    for k in range(CHUNKS):
        zcopy(k).start()
    for k in (0, 1, 2, 3):
        xcopy(0, 0, (0, 2, 1, 3)[k]).start()
        xcopy(0, 1, (1, 3, 0, 2)[k]).start()

    for i in range(3):
        loads[i].wait()
    gated = (gate_in[...].astype(f32) * values[...].astype(f32)).astype(bf16)
    SB[0] = gated.astype(f32).T.astype(bf16).reshape(SEQ_DEVS, OWN, BLOCK)
    SB[2] = filt[...].astype(f32).T.astype(bf16).reshape(SEQ_DEVS, OWN, BLOCK)
    loads[3].wait()
    goT[...] = gate_out[...].astype(f32).T
    acc[...] = jnp.zeros_like(acc)
    loads[4].wait()

    def multiply(q, step):
        h = block(q, step)

        def one(k, _):
            cols = pl.ds(pl.multiple_of(h * WIDTH + k * CW, CW), CW)
            acc[...] += nt(W[:, cols], G[h, k])
            return 0

        lax.fori_loop(0, CHUNKS, one, 0)

    def got(q, d, ks):
        for k in ks:
            xcopy(q, d, k, (-1, 1)[d]).wait_recv()

    def pass_on(q, d, k):
        got(q, d, (k,))
        fcopy(q, d, k, (-1, 1)[d]).start()

    def z_step(k):
        zcopy(k, 1).wait_recv()
        xcopy(1, 0, k).start()
        xcopy(1, 1, k).start()

    def finish_far(q):
        for k in (0, 2):
            fcopy(q, 0, k, 2).wait_recv()
        for k in (1, 3):
            fcopy(q, 1, k, 2).wait_recv()
        multiply(q, 2)

    pass_on(0, 0, 0)
    pass_on(0, 1, 1)
    pass_on(0, 0, 2)
    pass_on(0, 1, 3)
    z_step(0)
    multiply(0, 0)
    z_step(1)
    got(0, 0, (1, 3))
    multiply(0, -1)
    got(0, 1, (0, 2))
    multiply(0, 1)
    finish_far(0)
    pass_on(1, 0, 0)
    z_step(2)
    pass_on(1, 1, 1)
    z_step(3)
    multiply(1, 0)
    for f in (0, 2):
        spread_start(SB.at[f], XB.at[f], sa.at[f], ra.at[f])
        XB[f, pl.ds(s, 1)] = SB[f, pl.ds(s, 1)]
    pass_on(1, 0, 2)
    pass_on(1, 1, 3)
    got(1, 0, (1, 3))
    multiply(1, -1)
    got(1, 1, (0, 2))
    multiply(1, 1)
    finish_far(1)

    SB[1] = (acc[...] * goT[...]).astype(bf16).reshape(SEQ_DEVS, OWN, BLOCK)
    spread_start(SB.at[1], XB.at[1], sa.at[1], ra.at[1])
    XB[1, pl.ds(s, 1)] = SB[1, pl.ds(s, 1)]

    for i in range(5, 8):
        loads[i].wait()

    groups = ROWS // SEQ_DEVS
    t_re, t_im = turn_ref[0][None], turn_ref[1][None]

    def fold(a):
        return a.reshape(groups, SEQ_DEVS, BLOCK)

    def forward(f):
        def one(i, _):
            rows = pl.ds(pl.multiple_of(i * ROWS, ROWS), ROWS)
            rows_im = pl.ds(pl.multiple_of(CHANS + i * ROWS, ROWS), ROWS)
            data = XB[f].reshape(CHANS, BLOCK)
            re = fold(jnp.dot(first[rows, :], data, preferred_element_type=f32))
            im = fold(jnp.dot(first[rows_im, :], data, preferred_element_type=f32))
            z_re = (re * t_re - im * t_im).astype(bf16).reshape(ROWS, BLOCK)
            z_im = (re * t_im + im * t_re).astype(bf16).reshape(ROWS, BLOCK)
            Y[f, rows, :] = jnp.dot(
                z_re, second[:BLOCK, :], preferred_element_type=f32
            ) + jnp.dot(z_im, second[BLOCK:, :], preferred_element_type=f32)
            return 0

        lax.fori_loop(0, CHANS // ROWS, one, 0)

    def inverse(f, a, b):
        sign = 1.0 if f == 0 else -1.0

        def one(i, _):
            rows = pl.ds(pl.multiple_of(i * ROWS, ROWS), ROWS)
            rows_im = pl.ds(pl.multiple_of(CHANS + i * ROWS, ROWS), ROWS)
            a_re, a_im = Y[a, rows, :BLOCK], Y[a, rows, BLOCK:] * sign
            b_re, b_im = Y[b, rows, :BLOCK], Y[b, rows, BLOCK:]
            p_re = (a_re * b_re - a_im * b_im).astype(bf16)
            p_im = (a_re * b_im + a_im * b_re).astype(bf16)
            v = nt(p_re, second[:, :BLOCK]) + nt(p_im, second[:, BLOCK:])
            re, im = fold(v[:, :BLOCK]), fold(v[:, BLOCK:])
            Zs[rows, :] = (re * t_re + im * t_im).astype(bf16).reshape(ROWS, BLOCK)
            Zs[rows_im, :] = (im * t_re - re * t_im).astype(bf16).reshape(ROWS, BLOCK)
            return 0

        lax.fori_loop(0, CHANS // ROWS, one, 0)

        def two(i, _):
            rows = pl.ds(pl.multiple_of(i * ROWS, ROWS), ROWS)
            out = jnp.dot(last[rows, :], Zs[...], preferred_element_type=f32) * SCALE
            OB[f, pl.ds(i * (ROWS // OWN), ROWS // OWN)] = out.astype(bf16).reshape(ROWS // OWN, OWN, BLOCK)
            return 0

        lax.fori_loop(0, CHANS // ROWS, two, 0)
        spread_start(OB.at[f], RB.at[f], so.at[f], ro.at[f])
        RB[f, pl.ds(s, 1)] = OB[f, pl.ds(s, 1)]

    spread_wait(XB.at[0], ra.at[0])
    forward(0)
    spread_wait(XB.at[2], ra.at[2])
    forward(2)
    inverse(0, 2, 0)
    gz[...] = acc[...].T

    spread_wait(XB.at[1], ra.at[1])
    forward(1)
    inverse(1, 2, 1)
    inverse(2, 0, 1)

    total = jnp.sum(XB[0].astype(f32) * XB[1].astype(f32), axis=0)
    total = jnp.sum(total, axis=1, keepdims=True) * (1.0 / TOTAL)
    KS[...] = jnp.broadcast_to(total, KS.shape).astype(bf16)
    RS[pl.ds(s, 1)] = KS[...][None]

    def tell(i, _):
        d = lax.rem(s + i, SEQ_DEVS)
        remote(KS, RS.at[s], sk, rk, (d, c)).start()
        return 0

    lax.fori_loop(1, SEQ_DEVS, tell, 0)

    skip = skip_ref[...]
    gated = (gate_in[...].astype(f32) * values[...].astype(f32)).astype(bf16).astype(f32)

    def back(f):
        spread_wait(RB.at[f], ro.at[f])
        return RB[f].reshape(CHANS, BLOCK).astype(f32).T

    ggo_ref[...] = (gz[...] * (back(0) + skip * gated)).astype(bf16)
    grad_y = (gz[...] * gate_out[...].astype(f32)).astype(bf16).astype(f32)
    mixed = back(1) + skip * grad_y
    ggi_ref[...] = (mixed * values[...].astype(f32)).astype(bf16)
    gv_ref[...] = (mixed * gate_in[...].astype(f32)).astype(bf16)
    gf_ref[...] = back(2).astype(bf16)
    spread_wait(RS, rk)
    gs_ref[...] = RS[...].reshape(CHANS, 128)

    for q in range(2):
        for d in range(2):
            for k in range(CHUNKS):
                xcopy(q, d, k).wait_send()
            for k in (0, 2):
                fcopy(q, d, k + d, (-1, 1)[d]).wait_send()
    for k in range(CHUNKS):
        zcopy(k).wait_send()
    for f in range(3):
        spread_wait(SB.at[f], sa.at[f])
        spread_wait(OB.at[f], so.at[f])
    spread_wait(RS, sk)


def body(gate_out, gate_in, values, grad_out, w_out, filter_raw, skip):
    first, last, second, turn = tables()
    anyspace = pl.BlockSpec(memory_space=pl.ANY)
    vmem = pl.BlockSpec(memory_space=pltpu.VMEM)
    dma = pltpu.SemaphoreType.DMA
    field = (3, SEQ_DEVS, OWN, BLOCK)
    local = (BLOCK, CHANS)
    out = jax.ShapeDtypeStruct(local, bf16)
    outs = pl.pallas_call(
        kernel,
        out_shape=(out, out, out, out, jax.ShapeDtypeStruct((CHANS, 128), bf16)),
        in_specs=[anyspace] * 6 + [vmem] + [anyspace] * 3 + [vmem],
        out_specs=(vmem,) * 5,
        scratch_shapes=[
            pltpu.VMEM((CH_DEVS, CHUNKS, BLOCK, CW), bf16),
            pltpu.VMEM((CHANS, CH_DEVS * WIDTH), bf16),
            pltpu.VMEM((2 * CHANS, CHANS), bf16),
            pltpu.VMEM((CHANS, 2 * CHANS), bf16),
            pltpu.VMEM((2 * BLOCK, 2 * BLOCK), bf16),
            pltpu.VMEM(local, bf16),
            pltpu.VMEM(local, bf16),
            pltpu.VMEM(local, bf16),
            pltpu.VMEM(local, bf16),
            pltpu.VMEM((CHANS, BLOCK), f32),
            pltpu.VMEM(field, bf16),
            pltpu.VMEM(field, bf16),
            pltpu.VMEM(field, bf16),
            pltpu.VMEM(field, bf16),
            pltpu.VMEM((OWN, 128), bf16),
            pltpu.VMEM((SEQ_DEVS, OWN, 128), bf16),
            pltpu.VMEM((CHANS, BLOCK), f32),
            pltpu.VMEM(local, f32),
            pltpu.VMEM((3, CHANS, 2 * BLOCK), f32),
            pltpu.VMEM((2 * CHANS, BLOCK), bf16),
            dma((8,)),
            dma((CHUNKS,)),
            dma((2, 2, CHUNKS)),
            dma((2, 2, CHUNKS)),
            dma((2, 2, CHUNKS // 2)),
            dma((2, 2, CHUNKS // 2)),
            dma((CHUNKS,)),
            dma((CHUNKS,)),
            dma((3,)),
            dma((3,)),
            dma((3,)),
            dma((3,)),
            dma,
            dma,
        ],
        compiler_params=pltpu.CompilerParams(collective_id=0, has_side_effects=True, vmem_limit_bytes=48 << 20),
        name="hyena_backward",
    )(gate_out, gate_in, values, grad_out, w_out, filter_raw, skip[None, :], first, last, second, turn)
    return outs[:4] + (outs[4][:, 0],)


def solution(mesh):
    return jax.shard_map(
        body,
        mesh=mesh,
        in_specs=(
            P("seq", "ch"),
            P("seq", "ch"),
            P("seq", "ch"),
            P("seq", "ch"),
            P("ch", None),
            P("seq", "ch"),
            P("ch"),
        ),
        out_specs=(P("seq", "ch"), P("seq", "ch"), P("seq", "ch"), P("seq", "ch"), P("ch")),
        check_vma=False,
    )
```

```python
import functools
import math

import jax
import jax.numpy as jnp
import ml_dtypes
import numpy as np
from jax import lax
from jax.experimental import pallas as pl
from jax.experimental.pallas import tpu as pltpu
from jax.sharding import PartitionSpec as P

MESH = pl.DeviceIdType.MESH
bf16, f32 = jnp.bfloat16, jnp.float32

SEQ_DEVS = 32
CH_DEVS = 8
BLOCK = 256
CHANS = 512
OWN = CHANS // SEQ_DEVS
TOTAL = SEQ_DEVS * BLOCK
WIDTH = 1024
CHUNKS = 4
CR = BLOCK // CHUNKS
STEPS = 2
ROWS = 256
DEFER = 0
SCALE = 1.0 / (TOTAL * math.sqrt(TOTAL))


def tables():
    j = np.arange(SEQ_DEVS)
    ang = 2 * np.pi * (j[:, None] + 0.25) * j[None, :] / SEQ_DEVS
    eye = np.eye(OWN)
    parts = []
    for part in (np.cos(ang), -np.sin(ang)):
        parts.append(np.einsum("jp,ab->ajpb", part, eye).reshape(CHANS, CHANS))
    first = np.concatenate(parts, 0)
    m = np.arange(BLOCK)
    ang = 2 * np.pi * ((m[:, None] * m[None, :]) % BLOCK) / BLOCK
    cos, sin = np.cos(ang), np.sin(ang)
    second = np.block([[cos, -sin], [sin, cos]])
    ang = 2 * np.pi * (j[:, None] + 0.25) * m[None, :] / TOTAL
    turn = np.stack([np.cos(ang), -np.sin(ang)])
    cast = lambda a: a.astype(np.float32).astype(ml_dtypes.bfloat16)
    return cast(first), cast(first.T), cast(second), turn.astype(np.float32)


def nt(a, b):
    return lax.dot_general(a, b, (((1,), (1,)), ((), ())), preferred_element_type=f32)


def kernel(
    gate_out_hbm, gate_in_hbm, values_hbm, grad_out_hbm, w_hbm, filt_hbm, first_hbm, last_hbm, second_hbm, turn_ref,
    RB, RS, gz_ref,
    G, W, first, last, second, gate_out, gate_in, values, filt,
    goT, SB, XB, OB, KS, acc, gz, Y, Zs,
    lsem, ownsem, gsem, sx, rx, sf, rf, sz, rz, sa, ra, so, ro, sk, rk,
):
    s, c = lax.axis_index("seq"), lax.axis_index("ch")
    zbase = (c // 4) * 4
    x = lax.rem(c, 4)
    right, left, far = (s, zbase + lax.rem(x + 1, 4)), (s, zbase + lax.rem(x + 3, 4)), (s, lax.rem(c + 4, 8))

    def block(q, step):
        base = zbase if q == 0 else 4 - zbase
        return base + lax.rem(x + step + 4, 4)

    loads = [(gate_in_hbm, gate_in), (values_hbm, values), (filt_hbm, filt), (gate_out_hbm, gate_out), (w_hbm, W),
             (first_hbm, first), (second_hbm, second), (last_hbm, last)]
    own = pltpu.make_async_copy(grad_out_hbm, G.at[c], gsem)
    own.start()
    loads = [pltpu.make_async_copy(a, b, lsem.at[i]) for i, (a, b) in enumerate(loads)]
    for cp in loads:
        cp.start()

    barrier = pltpu.get_barrier_semaphore()
    for dev in (right, left, far):
        pl.semaphore_signal(barrier, inc=1, device_id=dev, device_id_type=MESH)

    def greet(i, _):
        pl.semaphore_signal(barrier, inc=1, device_id=(lax.rem(s + i, SEQ_DEVS), c), device_id_type=MESH)
        return 0

    lax.fori_loop(1, SEQ_DEVS, greet, 0)
    pl.semaphore_wait(barrier, SEQ_DEVS + 2)

    def remote(src, dst, ssem, rsem, dev):
        return pltpu.make_async_remote_copy(
            src_ref=src, dst_ref=dst, send_sem=ssem, recv_sem=rsem, device_id=dev, device_id_type=MESH
        )

    def xcopy(q, d, k, step=0):
        ref = G.at[block(q, step), pl.ds(k * CR, CR)]
        return remote(ref, ref, sx.at[q, d, k], rx.at[q, d, k], (right, left)[d])

    def fcopy(q, d, k, step):
        ref = G.at[block(q, step), pl.ds(k * CR, CR)]
        return remote(ref, ref, sf.at[q, d, k // 2], rf.at[q, d, k // 2], (right, left)[d])

    def zcopy(k, q=0):
        ref = G.at[block(q, 0), pl.ds(k * CR, CR)]
        return remote(ref, ref, sz.at[k], rz.at[k], far)

    def spread_start(buf, dst, ssem, rsem, tail=()):
        def one(i, _):
            d = lax.rem(s + i, SEQ_DEVS)
            remote(buf.at[d], dst.at[s], ssem, rsem, (d, c)).start()
            return 0

        lax.fori_loop(1, SEQ_DEVS, one, 0)

    def spread_wait(buf, sem):
        part = buf.at[pl.ds(0, SEQ_DEVS - 1)]
        pltpu.make_async_copy(part, part, sem).wait()

    even, odd = tuple(range(0, CHUNKS, 2)), tuple(range(1, CHUNKS, 2))
    own.wait()
    for k in range(CHUNKS):
        zcopy(k).start()
    for a, b in zip(even, odd):
        xcopy(0, 0, a).start()
        xcopy(0, 1, b).start()
    for a, b in zip(even, odd):
        xcopy(0, 0, b).start()
        xcopy(0, 1, a).start()

    def send_field(f, columns):
        SB[f] = columns.T.astype(bf16).reshape(SEQ_DEVS, OWN, BLOCK)
        spread_start(SB.at[f], XB.at[f], sa.at[f], ra.at[f])
        XB[f, pl.ds(s, 1)] = SB[f, pl.ds(s, 1)]

    for i in (0, 1, 3, 4):
        loads[i].wait()
    gated = (gate_in[...].astype(f32) * values[...].astype(f32)).astype(bf16)
    goT[...] = gate_out[...].astype(f32).T

    def multiply(q, step, begin=False):
        h = block(q, step)
        cols = pl.ds(pl.multiple_of(h * WIDTH, WIDTH), WIDTH)
        part = nt(W[:, cols], G[h])
        acc[...] = part if begin else acc[...] + part

    def got(q, d, ks):
        for k in ks:
            xcopy(q, d, k, (-1, 1)[d]).wait_recv()

    def pass_on(q, d, k):
        got(q, d, (k,))
        fcopy(q, d, k, (-1, 1)[d]).start()

    def z_step(k):
        if k < CHUNKS:
            zcopy(k, 1).wait_recv()
            xcopy(1, k % 2, k).start()
        if 0 <= k - DEFER < CHUNKS:
            xcopy(1, 1 - k % 2, k - DEFER).start()

    def finish_side(q, d):
        got(q, d, (odd, even)[d])
        multiply(q, (-1, 1)[d])

    def finish_far(q):
        for k in even:
            fcopy(q, 0, k, 2).wait_recv()
        for k in odd:
            fcopy(q, 1, k, 2).wait_recv()
        multiply(q, 2)

    groups = ROWS // SEQ_DEVS
    t_re, t_im = turn_ref[0][None], turn_ref[1][None]

    def fold(a):
        return a.reshape(groups, SEQ_DEVS, BLOCK)

    def forward(f):
        def one(i, _):
            rows = pl.ds(pl.multiple_of(i * ROWS, ROWS), ROWS)
            rows_im = pl.ds(pl.multiple_of(CHANS + i * ROWS, ROWS), ROWS)
            data = XB[f].reshape(CHANS, BLOCK)
            re = fold(jnp.dot(first[rows, :], data, preferred_element_type=f32))
            im = fold(jnp.dot(first[rows_im, :], data, preferred_element_type=f32))
            z_re = (re * t_re - im * t_im).astype(bf16).reshape(ROWS, BLOCK)
            z_im = (re * t_im + im * t_re).astype(bf16).reshape(ROWS, BLOCK)
            Y[f, rows, :] = jnp.dot(
                z_re, second[:BLOCK, :], preferred_element_type=f32
            ) + jnp.dot(z_im, second[BLOCK:, :], preferred_element_type=f32)
            return 0

        lax.fori_loop(0, CHANS // ROWS, one, 0)

    def inverse(f, a, b):
        sign = 1.0 if f == 0 else -1.0

        def one(i, _):
            rows = pl.ds(pl.multiple_of(i * ROWS, ROWS), ROWS)
            rows_im = pl.ds(pl.multiple_of(CHANS + i * ROWS, ROWS), ROWS)
            a_re, a_im = Y[a, rows, :BLOCK], Y[a, rows, BLOCK:] * sign
            b_re, b_im = Y[b, rows, :BLOCK], Y[b, rows, BLOCK:]
            p_re = (a_re * b_re - a_im * b_im).astype(bf16)
            p_im = (a_re * b_im + a_im * b_re).astype(bf16)
            v = nt(p_re, second[:, :BLOCK]) + nt(p_im, second[:, BLOCK:])
            re, im = fold(v[:, :BLOCK]), fold(v[:, BLOCK:])
            Zs[rows, :] = (re * t_re + im * t_im).astype(bf16).reshape(ROWS, BLOCK)
            Zs[rows_im, :] = (im * t_re - re * t_im).astype(bf16).reshape(ROWS, BLOCK)
            return 0

        lax.fori_loop(0, CHANS // ROWS, one, 0)

        def two(i, _):
            rows = pl.ds(pl.multiple_of(i * ROWS, ROWS), ROWS)
            out = jnp.dot(last[rows, :], Zs[...], preferred_element_type=f32) * SCALE
            OB[f, pl.ds(i * (ROWS // OWN), ROWS // OWN)] = out.astype(bf16).reshape(ROWS // OWN, OWN, BLOCK)
            return 0

        lax.fori_loop(0, CHANS // ROWS, two, 0)
        spread_start(OB.at[f], RB.at[f], so.at[f], ro.at[f])
        pltpu.make_async_copy(OB.at[f, s], RB.at[f, s], ownsem.at[f]).start()

    loads[2].wait()
    multiply(0, 0, begin=True)
    pass_on(0, 0, 0)
    pass_on(0, 1, 1)
    z_step(0)
    pass_on(0, 0, 2)
    pass_on(0, 1, 3)
    z_step(1)
    finish_side(0, 0)
    finish_side(0, 1)
    z_step(2)
    pass_on(1, 0, 0)
    pass_on(1, 1, 1)
    finish_far(0)
    z_step(3)
    send_field(2, filt[...].astype(f32))
    send_field(0, gated.astype(f32))
    multiply(1, 0)
    for i in range(5, 8):
        loads[i].wait()
    pass_on(1, 0, 2)
    pass_on(1, 1, 3)
    finish_side(1, 0)
    finish_side(1, 1)
    finish_far(1)
    SB[1] = (acc[...] * goT[...]).astype(bf16).reshape(SEQ_DEVS, OWN, BLOCK)
    spread_start(SB.at[1], XB.at[1], sa.at[1], ra.at[1])
    XB[1, pl.ds(s, 1)] = SB[1, pl.ds(s, 1)]
    spread_wait(XB.at[2], ra.at[2])
    forward(2)
    spread_wait(XB.at[0], ra.at[0])
    forward(0)
    inverse(0, 2, 0)
    gz[...] = acc[...].T
    pltpu.make_async_copy(gz, gz_ref, ownsem.at[4]).start()

    spread_wait(XB.at[1], ra.at[1])
    forward(1)
    inverse(1, 2, 1)
    inverse(2, 0, 1)

    total = jnp.sum(XB[0].astype(f32) * XB[1].astype(f32), axis=0)
    total = jnp.sum(total, axis=1, keepdims=True) * (1.0 / TOTAL)
    here = lax.rem(lax.broadcasted_iota(jnp.int32, (OWN, 128), 1), OWN) == lax.broadcasted_iota(jnp.int32, (OWN, 128), 0)
    KS[...] = jnp.sum(jnp.where(here, total, 0.0), axis=0, keepdims=True)
    pltpu.make_async_copy(KS, RS.at[s], ownsem.at[3]).start()

    def tell(i, _):
        d = lax.rem(s + i, SEQ_DEVS)
        remote(KS, RS.at[s], sk, rk, (d, c)).start()
        return 0

    lax.fori_loop(1, SEQ_DEVS, tell, 0)

    for f in range(3):
        spread_wait(RB.at[f], ro.at[f])
        pltpu.make_async_copy(OB.at[f, s], RB.at[f, s], ownsem.at[f]).wait()
    spread_wait(RS, rk)
    pltpu.make_async_copy(KS, RS.at[s], ownsem.at[3]).wait()
    pltpu.make_async_copy(gz, gz_ref, ownsem.at[4]).wait()

    for q in range(2):
        for d in range(2):
            for k in range(CHUNKS):
                xcopy(q, d, k).wait_send()
            for k in (even, odd)[d]:
                fcopy(q, d, k, (-1, 1)[d]).wait_send()
    for k in range(CHUNKS):
        zcopy(k).wait_send()
    for f in range(3):
        spread_wait(SB.at[f], sa.at[f])
        spread_wait(OB.at[f], so.at[f])
    spread_wait(RS, sk)


def finish(back_ref, sums_ref, gz_ref, gate_out_ref, gate_in_ref, values_ref, skip_ref, ggo_ref, ggi_ref, gv_ref, gf_ref, gs_ref):
    def back(f):
        return back_ref[f].reshape(-1, BLOCK).astype(f32).T

    skip, gz = skip_ref[...], gz_ref[...]
    gate_in, values = gate_in_ref[...].astype(f32), values_ref[...].astype(f32)
    gated = (gate_in * values).astype(bf16).astype(f32)
    ggo_ref[...] = (gz * (back(0) + skip * gated)).astype(bf16)
    grad_y = (gz * gate_out_ref[...].astype(f32)).astype(bf16).astype(f32)
    mixed = back(1) + skip * grad_y
    ggi_ref[...] = (mixed * values).astype(bf16)
    gv_ref[...] = (mixed * gate_in).astype(bf16)
    gf_ref[...] = back(2).astype(bf16)

    @pl.when(pl.program_id(0) == 0)
    def _():
        sums = jnp.concatenate([sums_ref[:, 0, :]] * (CHANS // 128), axis=1)
        device = lax.broadcasted_iota(jnp.int32, sums.shape, 1) // OWN
        keep = device == lax.broadcasted_iota(jnp.int32, sums.shape, 0)
        gs_ref[...] = jnp.sum(jnp.where(keep, sums, 0.0), axis=0).astype(bf16)


def body(gate_out, gate_in, values, grad_out, w_out, filter_raw, skip):
    first, last, second, turn = tables()
    anyspace = pl.BlockSpec(memory_space=pl.ANY)
    hbm = pl.BlockSpec(memory_space=pltpu.HBM)
    vmem = pl.BlockSpec(memory_space=pltpu.VMEM)
    dma = pltpu.SemaphoreType.DMA
    field = (3, SEQ_DEVS, OWN, BLOCK)
    local = (BLOCK, CHANS)
    back, sums, grad_z = pl.pallas_call(
        kernel,
        out_shape=(
            jax.ShapeDtypeStruct(field, bf16),
            jax.ShapeDtypeStruct((SEQ_DEVS, 1, 128), f32),
            jax.ShapeDtypeStruct(local, f32),
        ),
        in_specs=[hbm] * 6 + [anyspace] * 3 + [vmem],
        out_specs=(hbm,) * 3,
        scratch_shapes=[
            pltpu.VMEM((CH_DEVS, BLOCK, WIDTH), bf16),
            pltpu.VMEM((CHANS, CH_DEVS * WIDTH), bf16),
            pltpu.VMEM((2 * CHANS, CHANS), bf16),
            pltpu.VMEM((CHANS, 2 * CHANS), bf16),
            pltpu.VMEM((2 * BLOCK, 2 * BLOCK), bf16),
            pltpu.VMEM(local, bf16),
            pltpu.VMEM(local, bf16),
            pltpu.VMEM(local, bf16),
            pltpu.VMEM(local, bf16),
            pltpu.VMEM((CHANS, BLOCK), f32),
            pltpu.VMEM(field, bf16),
            pltpu.VMEM(field, bf16),
            pltpu.VMEM(field, bf16),
            pltpu.VMEM((1, 128), f32),
            pltpu.VMEM((CHANS, BLOCK), f32),
            pltpu.VMEM(local, f32),
            pltpu.VMEM((3, CHANS, 2 * BLOCK), f32),
            pltpu.VMEM((2 * CHANS, BLOCK), bf16),
            dma((8,)),
            dma((5,)),
            dma,
            dma((2, 2, CHUNKS)),
            dma((2, 2, CHUNKS)),
            dma((2, 2, CHUNKS // 2)),
            dma((2, 2, CHUNKS // 2)),
            dma((CHUNKS,)),
            dma((CHUNKS,)),
            dma((3,)),
            dma((3,)),
            dma((3,)),
            dma((3,)),
            dma,
            dma,
        ],
        compiler_params=pltpu.CompilerParams(collective_id=0, has_side_effects=True, vmem_limit_bytes=60 << 20),
        name="transforms",
    )(gate_out, gate_in, values, grad_out, w_out, filter_raw, first, last, second, turn)
    out = jax.ShapeDtypeStruct(local, bf16)
    cols = CHANS // STEPS
    tile = pl.BlockSpec((BLOCK, cols), lambda i: (0, i))
    row = pl.BlockSpec((1, cols), lambda i: (0, i))
    outs = pl.pallas_call(
        finish,
        grid=(STEPS,),
        out_shape=(out, out, out, out, jax.ShapeDtypeStruct((CHANS,), bf16)),
        in_specs=[
            pl.BlockSpec((3, SEQ_DEVS // STEPS, OWN, BLOCK), lambda i: (0, i, 0, 0)),
            pl.BlockSpec((SEQ_DEVS, 1, 128), lambda i: (0, 0, 0)),
            tile,
            tile,
            tile,
            tile,
            row,
        ],
        out_specs=(tile, tile, tile, tile, pl.BlockSpec((CHANS,), lambda i: (0,))),
        compiler_params=pltpu.CompilerParams(vmem_limit_bytes=60 << 20),
        name="gradients",
    )(back, sums, grad_z, gate_out, gate_in, values, skip[None, :])
    return outs


def solution(mesh):
    return jax.shard_map(
        body,
        mesh=mesh,
        in_specs=(
            P("seq", "ch"),
            P("seq", "ch"),
            P("seq", "ch"),
            P("seq", "ch"),
            P("ch", None),
            P("seq", "ch"),
            P("ch"),
        ),
        out_specs=(P("seq", "ch"), P("seq", "ch"), P("seq", "ch"), P("seq", "ch"), P("ch")),
        check_vma=False,
    )
```

```python
import functools
import math

import jax
import jax.numpy as jnp
import ml_dtypes
import numpy as np
from jax import lax
from jax.experimental import pallas as pl
from jax.experimental.pallas import tpu as pltpu
from jax.sharding import PartitionSpec as P

MESH = pl.DeviceIdType.MESH
bf16, f32 = jnp.bfloat16, jnp.float32

SEQ_DEVS = 32
CH_DEVS = 8
BLOCK = 256
CHANS = 512
OWN = CHANS // SEQ_DEVS
TOTAL = SEQ_DEVS * BLOCK
WIDTH = 1024
CHUNKS = 4
CR = BLOCK // CHUNKS
HALF = BLOCK // 2
STEPS = 2
ROWS = 256
DEFER = 0
SCALE = 1.0 / (TOTAL * math.sqrt(TOTAL))


def tables():
    j = np.arange(SEQ_DEVS)
    ang = 2 * np.pi * (j[:, None] + 0.25) * j[None, :] / SEQ_DEVS
    eye = np.eye(OWN)
    parts = []
    for part in (np.cos(ang), -np.sin(ang)):
        parts.append(np.einsum("jp,ab->ajpb", part, eye).reshape(CHANS, CHANS))
    first = np.concatenate(parts, 0)
    m = np.arange(BLOCK)
    ang = 2 * np.pi * ((m[:, None] * m[None, :]) % BLOCK) / BLOCK
    cos, sin = np.cos(ang), np.sin(ang)
    second = np.block([[cos, -sin], [sin, cos]])
    ang = 2 * np.pi * (j[:, None] + 0.25) * m[None, :] / TOTAL
    turn = np.stack([np.cos(ang), -np.sin(ang)])
    cast = lambda a: a.astype(np.float32).astype(ml_dtypes.bfloat16)
    return cast(first), cast(first.T), cast(second), turn.astype(np.float32)


def nt(a, b):
    return lax.dot_general(a, b, (((1,), (1,)), ((), ())), preferred_element_type=f32)


def kernel(
    gate_out_hbm, gate_in_hbm, values_hbm, grad_out_hbm, w_hbm, filt_hbm, first_hbm, last_hbm, second_hbm, turn_ref,
    RB, RS, gz_ref,
    G, W, first, last, second, gate_out, gate_in, values, filt,
    goT, SB, XB, SD, XD, OB, KS, acc, gz, Y, Zs,
    lsem, ownsem, gsem, sx, rx, sf, rf, sz, rz, sa, ra, sd, rd, so, ro, sk, rk,
):
    s, c = lax.axis_index("seq"), lax.axis_index("ch")
    zbase = (c // 4) * 4
    x = lax.rem(c, 4)
    right, left, far = (s, zbase + lax.rem(x + 1, 4)), (s, zbase + lax.rem(x + 3, 4)), (s, lax.rem(c + 4, 8))

    def block(q, step):
        base = zbase if q == 0 else 4 - zbase
        return base + lax.rem(x + step + 4, 4)

    loads = [(gate_in_hbm, gate_in), (values_hbm, values), (filt_hbm, filt), (gate_out_hbm, gate_out), (w_hbm, W),
             (first_hbm, first), (second_hbm, second), (last_hbm, last)]
    own = pltpu.make_async_copy(grad_out_hbm, G.at[c], gsem)
    own.start()
    loads = [pltpu.make_async_copy(a, b, lsem.at[i]) for i, (a, b) in enumerate(loads)]
    for cp in loads[:4]:
        cp.start()

    barrier = pltpu.get_barrier_semaphore()
    for dev in (right, left, far):
        pl.semaphore_signal(barrier, inc=1, device_id=dev, device_id_type=MESH)

    def greet(i, _):
        pl.semaphore_signal(barrier, inc=1, device_id=(lax.rem(s + i, SEQ_DEVS), c), device_id_type=MESH)
        return 0

    lax.fori_loop(1, SEQ_DEVS, greet, 0)
    pl.semaphore_wait(barrier, SEQ_DEVS + 2)

    def remote(src, dst, ssem, rsem, dev):
        return pltpu.make_async_remote_copy(
            src_ref=src, dst_ref=dst, send_sem=ssem, recv_sem=rsem, device_id=dev, device_id_type=MESH
        )

    def xcopy(q, d, k, step=0):
        ref = G.at[block(q, step), pl.ds(k * CR, CR)]
        return remote(ref, ref, sx.at[q, d, k], rx.at[q, d, k], (right, left)[d])

    def fcopy(q, d, k, step):
        ref = G.at[block(q, step), pl.ds(k * CR, CR)]
        return remote(ref, ref, sf.at[q, d, k // 2], rf.at[q, d, k // 2], (right, left)[d])

    def zcopy(k, q=0):
        ref = G.at[block(q, 0), pl.ds(k * CR, CR)]
        return remote(ref, ref, sz.at[k], rz.at[k], far)

    def spread_start(buf, dst, ssem, rsem, tail=()):
        def one(i, _):
            d = lax.rem(s + i, SEQ_DEVS)
            remote(buf.at[d], dst.at[s], ssem, rsem, (d, c)).start()
            return 0

        lax.fori_loop(1, SEQ_DEVS, one, 0)

    def spread_wait(buf, sem):
        part = buf.at[pl.ds(0, SEQ_DEVS - 1)]
        pltpu.make_async_copy(part, part, sem).wait()

    even, odd = tuple(range(0, CHUNKS, 2)), tuple(range(1, CHUNKS, 2))
    own.wait()
    for a, b in zip(even, odd):
        xcopy(0, 0, a).start()
        xcopy(0, 1, b).start()
    for k in range(CHUNKS):
        zcopy(k).start()
    for cp in loads[4:]:
        cp.start()

    def send_field(f, columns):
        SB[f] = columns.T.astype(bf16).reshape(SEQ_DEVS, OWN, BLOCK)
        spread_start(SB.at[f], XB.at[f], sa.at[f], ra.at[f])
        XB[f, pl.ds(s, 1)] = SB[f, pl.ds(s, 1)]

    for i in (0, 1, 3, 4):
        loads[i].wait()
    gated = (gate_in[...].astype(f32) * values[...].astype(f32)).astype(bf16)
    goT[...] = gate_out[...].astype(f32).T

    def multiply(q, step, begin=False):
        h = block(q, step)
        cols = pl.ds(pl.multiple_of(h * WIDTH, WIDTH), WIDTH)
        part = nt(W[:, cols], G[h])
        acc[...] = part if begin else acc[...] + part

    def multiply_half(step, half):
        h = block(1, step)
        cols = pl.ds(pl.multiple_of(h * WIDTH, WIDTH), WIDTH)
        rows = slice(half * HALF, (half + 1) * HALF)
        acc[:, rows] += nt(W[:, cols], G[h, rows])

    def half_done(half):
        lo = half * CHUNKS // 2
        ks = range(lo, lo + CHUNKS // 2)
        multiply_half(0, half)
        for d in range(2):
            got(1, d, [k for k in ks if k % 2 != d])
            multiply_half((-1, 1)[d], half)
        for k in ks:
            fcopy(1, k % 2, k, 2).wait_recv()
        multiply_half(2, half)

    def send_half(half):
        rows = slice(half * HALF, (half + 1) * HALF)
        SD[half] = (acc[:, rows] * goT[:, rows]).astype(bf16).reshape(SEQ_DEVS, OWN, HALF)
        spread_start(SD.at[half], XD.at[half], sd.at[half], rd.at[half])
        XD[half, pl.ds(s, 1)] = SD[half, pl.ds(s, 1)]

    def got(q, d, ks):
        for k in ks:
            xcopy(q, d, k, (-1, 1)[d]).wait_recv()

    def pass_on(q, d, k):
        got(q, d, (k,))
        fcopy(q, d, k, (-1, 1)[d]).start()

    def z_step(k):
        if k < CHUNKS:
            zcopy(k, 1).wait_recv()
            xcopy(1, k % 2, k).start()
        if 0 <= k - DEFER < CHUNKS:
            xcopy(1, 1 - k % 2, k - DEFER).start()

    def finish_side(q, d):
        got(q, d, (odd, even)[d])
        multiply(q, (-1, 1)[d])

    def finish_far(q):
        for k in even:
            fcopy(q, 0, k, 2).wait_recv()
        for k in odd:
            fcopy(q, 1, k, 2).wait_recv()
        multiply(q, 2)

    groups = ROWS // SEQ_DEVS
    t_re, t_im = turn_ref[0][None], turn_ref[1][None]

    def fold(a):
        return a.reshape(groups, SEQ_DEVS, BLOCK)

    def both():
        return jnp.concatenate([XD[half].reshape(CHANS, HALF) for half in range(2)], axis=1)

    def forward(f):
        def one(i, _):
            rows = pl.ds(pl.multiple_of(i * ROWS, ROWS), ROWS)
            rows_im = pl.ds(pl.multiple_of(CHANS + i * ROWS, ROWS), ROWS)
            data = XB[f].reshape(CHANS, BLOCK) if f < 2 else both()
            re = fold(jnp.dot(first[rows, :], data, preferred_element_type=f32))
            im = fold(jnp.dot(first[rows_im, :], data, preferred_element_type=f32))
            z_re = (re * t_re - im * t_im).astype(bf16).reshape(ROWS, BLOCK)
            z_im = (re * t_im + im * t_re).astype(bf16).reshape(ROWS, BLOCK)
            Y[f, rows, :] = jnp.dot(
                z_re, second[:BLOCK, :], preferred_element_type=f32
            ) + jnp.dot(z_im, second[BLOCK:, :], preferred_element_type=f32)
            return 0

        lax.fori_loop(0, CHANS // ROWS, one, 0)

    def inverse(f, a, b):
        sign = 1.0 if f == 0 else -1.0

        def one(i, _):
            rows = pl.ds(pl.multiple_of(i * ROWS, ROWS), ROWS)
            rows_im = pl.ds(pl.multiple_of(CHANS + i * ROWS, ROWS), ROWS)
            a_re, a_im = Y[a, rows, :BLOCK], Y[a, rows, BLOCK:] * sign
            b_re, b_im = Y[b, rows, :BLOCK], Y[b, rows, BLOCK:]
            p_re = (a_re * b_re - a_im * b_im).astype(bf16)
            p_im = (a_re * b_im + a_im * b_re).astype(bf16)
            v = nt(p_re, second[:, :BLOCK]) + nt(p_im, second[:, BLOCK:])
            re, im = fold(v[:, :BLOCK]), fold(v[:, BLOCK:])
            Zs[rows, :] = (re * t_re + im * t_im).astype(bf16).reshape(ROWS, BLOCK)
            Zs[rows_im, :] = (im * t_re - re * t_im).astype(bf16).reshape(ROWS, BLOCK)
            return 0

        lax.fori_loop(0, CHANS // ROWS, one, 0)

        def two(i, _):
            rows = pl.ds(pl.multiple_of(i * ROWS, ROWS), ROWS)
            out = jnp.dot(last[rows, :], Zs[...], preferred_element_type=f32) * SCALE
            OB[f, pl.ds(i * (ROWS // OWN), ROWS // OWN)] = out.astype(bf16).reshape(ROWS // OWN, OWN, BLOCK)
            return 0

        lax.fori_loop(0, CHANS // ROWS, two, 0)
        spread_start(OB.at[f], RB.at[f], so.at[f], ro.at[f])
        pltpu.make_async_copy(OB.at[f, s], RB.at[f, s], ownsem.at[f]).start()

    loads[2].wait()
    send_field(1, filt[...].astype(f32))
    multiply(0, 0, begin=True)
    pass_on(0, 0, 0)
    pass_on(0, 1, 1)
    xcopy(0, 0, 1).start()
    xcopy(0, 1, 0).start()
    z_step(0)
    pass_on(0, 0, 2)
    pass_on(0, 1, 3)
    xcopy(0, 0, 3).start()
    xcopy(0, 1, 2).start()
    z_step(1)
    finish_side(0, 0)
    finish_side(0, 1)
    z_step(2)
    pass_on(1, 0, 0)
    pass_on(1, 1, 1)
    finish_far(0)
    z_step(3)
    send_field(0, gated.astype(f32))
    half_done(0)
    pass_on(1, 0, 2)
    pass_on(1, 1, 3)
    send_half(0)
    half_done(1)
    send_half(1)
    for i in range(5, 8):
        loads[i].wait()
    spread_wait(XB.at[1], ra.at[1])
    forward(1)
    spread_wait(XB.at[0], ra.at[0])
    forward(0)
    inverse(0, 1, 0)

    gz[...] = acc[...].T
    pltpu.make_async_copy(gz, gz_ref, ownsem.at[4]).start()

    for half in range(2):
        spread_wait(XD.at[half], rd.at[half])
    forward(2)
    inverse(1, 1, 2)
    inverse(2, 0, 2)

    total = jnp.sum(XB[0].astype(f32) * both().reshape(XB.shape[1:]).astype(f32), axis=0)
    total = jnp.sum(total, axis=1, keepdims=True) * (1.0 / TOTAL)
    here = lax.rem(lax.broadcasted_iota(jnp.int32, (OWN, 128), 1), OWN) == lax.broadcasted_iota(jnp.int32, (OWN, 128), 0)
    KS[...] = jnp.sum(jnp.where(here, total, 0.0), axis=0, keepdims=True)
    pltpu.make_async_copy(KS, RS.at[s], ownsem.at[3]).start()

    def tell(i, _):
        d = lax.rem(s + i, SEQ_DEVS)
        remote(KS, RS.at[s], sk, rk, (d, c)).start()
        return 0

    lax.fori_loop(1, SEQ_DEVS, tell, 0)

    for f in range(3):
        spread_wait(RB.at[f], ro.at[f])
        pltpu.make_async_copy(OB.at[f, s], RB.at[f, s], ownsem.at[f]).wait()
    spread_wait(RS, rk)
    pltpu.make_async_copy(KS, RS.at[s], ownsem.at[3]).wait()
    pltpu.make_async_copy(gz, gz_ref, ownsem.at[4]).wait()

    for q in range(2):
        for d in range(2):
            for k in range(CHUNKS):
                xcopy(q, d, k).wait_send()
            for k in (even, odd)[d]:
                fcopy(q, d, k, (-1, 1)[d]).wait_send()
    for k in range(CHUNKS):
        zcopy(k).wait_send()
    for f in range(2):
        spread_wait(SB.at[f], sa.at[f])
        spread_wait(SD.at[f], sd.at[f])
    for f in range(3):
        spread_wait(OB.at[f], so.at[f])
    spread_wait(RS, sk)


def finish(back_ref, sums_ref, gz_ref, gate_out_ref, gate_in_ref, values_ref, skip_ref, ggo_ref, ggi_ref, gv_ref, gf_ref, gs_ref):
    def back(f):
        return back_ref[f].reshape(-1, BLOCK).astype(f32).T

    skip, gz = skip_ref[...], gz_ref[...]
    gate_in, values = gate_in_ref[...].astype(f32), values_ref[...].astype(f32)
    gated = (gate_in * values).astype(bf16).astype(f32)
    ggo_ref[...] = (gz * (back(0) + skip * gated)).astype(bf16)
    grad_y = (gz * gate_out_ref[...].astype(f32)).astype(bf16).astype(f32)
    mixed = back(1) + skip * grad_y
    ggi_ref[...] = (mixed * values).astype(bf16)
    gv_ref[...] = (mixed * gate_in).astype(bf16)
    gf_ref[...] = back(2).astype(bf16)

    @pl.when(pl.program_id(0) == 0)
    def _():
        sums = jnp.concatenate([sums_ref[:, 0, :]] * (CHANS // 128), axis=1)
        device = lax.broadcasted_iota(jnp.int32, sums.shape, 1) // OWN
        keep = device == lax.broadcasted_iota(jnp.int32, sums.shape, 0)
        gs_ref[...] = jnp.sum(jnp.where(keep, sums, 0.0), axis=0).astype(bf16)


def body(gate_out, gate_in, values, grad_out, w_out, filter_raw, skip):
    first, last, second, turn = tables()
    anyspace = pl.BlockSpec(memory_space=pl.ANY)
    hbm = pl.BlockSpec(memory_space=pltpu.HBM)
    vmem = pl.BlockSpec(memory_space=pltpu.VMEM)
    dma = pltpu.SemaphoreType.DMA
    field = (3, SEQ_DEVS, OWN, BLOCK)
    local = (BLOCK, CHANS)
    back, sums, grad_z = pl.pallas_call(
        kernel,
        out_shape=(
            jax.ShapeDtypeStruct(field, bf16),
            jax.ShapeDtypeStruct((SEQ_DEVS, 1, 128), f32),
            jax.ShapeDtypeStruct(local, f32),
        ),
        in_specs=[hbm] * 6 + [anyspace] * 3 + [vmem],
        out_specs=(hbm,) * 3,
        scratch_shapes=[
            pltpu.VMEM((CH_DEVS, BLOCK, WIDTH), bf16),
            pltpu.VMEM((CHANS, CH_DEVS * WIDTH), bf16),
            pltpu.VMEM((2 * CHANS, CHANS), bf16),
            pltpu.VMEM((CHANS, 2 * CHANS), bf16),
            pltpu.VMEM((2 * BLOCK, 2 * BLOCK), bf16),
            pltpu.VMEM(local, bf16),
            pltpu.VMEM(local, bf16),
            pltpu.VMEM(local, bf16),
            pltpu.VMEM(local, bf16),
            pltpu.VMEM((CHANS, BLOCK), f32),
            pltpu.VMEM((2,) + field[1:], bf16),
            pltpu.VMEM((2,) + field[1:], bf16),
            pltpu.VMEM((2, SEQ_DEVS, OWN, HALF), bf16),
            pltpu.VMEM((2, SEQ_DEVS, OWN, HALF), bf16),
            pltpu.VMEM(field, bf16),
            pltpu.VMEM((1, 128), f32),
            pltpu.VMEM((CHANS, BLOCK), f32),
            pltpu.VMEM(local, f32),
            pltpu.VMEM((3, CHANS, 2 * BLOCK), f32),
            pltpu.VMEM((2 * CHANS, BLOCK), bf16),
            dma((8,)),
            dma((5,)),
            dma,
            dma((2, 2, CHUNKS)),
            dma((2, 2, CHUNKS)),
            dma((2, 2, CHUNKS // 2)),
            dma((2, 2, CHUNKS // 2)),
            dma((CHUNKS,)),
            dma((CHUNKS,)),
            dma((2,)),
            dma((2,)),
            dma((2,)),
            dma((2,)),
            dma((3,)),
            dma((3,)),
            dma,
            dma,
        ],
        compiler_params=pltpu.CompilerParams(collective_id=0, has_side_effects=True, vmem_limit_bytes=60 << 20),
        name="transforms",
    )(gate_out, gate_in, values, grad_out, w_out, filter_raw, first, last, second, turn)
    out = jax.ShapeDtypeStruct(local, bf16)
    cols = CHANS // STEPS
    tile = pl.BlockSpec((BLOCK, cols), lambda i: (0, i))
    row = pl.BlockSpec((1, cols), lambda i: (0, i))
    outs = pl.pallas_call(
        finish,
        grid=(STEPS,),
        out_shape=(out, out, out, out, jax.ShapeDtypeStruct((CHANS,), bf16)),
        in_specs=[
            pl.BlockSpec((3, SEQ_DEVS // STEPS, OWN, BLOCK), lambda i: (0, i, 0, 0)),
            pl.BlockSpec((SEQ_DEVS, 1, 128), lambda i: (0, 0, 0)),
            tile,
            tile,
            tile,
            tile,
            row,
        ],
        out_specs=(tile, tile, tile, tile, pl.BlockSpec((CHANS,), lambda i: (0,))),
        compiler_params=pltpu.CompilerParams(vmem_limit_bytes=60 << 20),
        name="gradients",
    )(back, sums, grad_z, gate_out, gate_in, values, skip[None, :])
    return outs


def solution(mesh):
    return jax.shard_map(
        body,
        mesh=mesh,
        in_specs=(
            P("seq", "ch"),
            P("seq", "ch"),
            P("seq", "ch"),
            P("seq", "ch"),
            P("ch", None),
            P("seq", "ch"),
            P("ch"),
        ),
        out_specs=(P("seq", "ch"), P("seq", "ch"), P("seq", "ch"), P("seq", "ch"), P("ch")),
        check_vma=False,
    )
```

```python
import functools
import math

import jax
import jax.numpy as jnp
import ml_dtypes
import numpy as np
from jax import lax
from jax.experimental import pallas as pl
from jax.experimental.pallas import tpu as pltpu
from jax.sharding import PartitionSpec as P

MESH = pl.DeviceIdType.MESH
bf16, f32 = jnp.bfloat16, jnp.float32

SEQ_DEVS = 32
CH_DEVS = 8
BLOCK = 256
CHANS = 512
OWN = CHANS // SEQ_DEVS
TOTAL = SEQ_DEVS * BLOCK
WIDTH = 1024
CHUNKS = 4
CR = BLOCK // CHUNKS
HALF = BLOCK // 2
STEPS = 2
ROWS = 256
DEFER = 0
SCALE = 1.0 / (TOTAL * math.sqrt(TOTAL))


def tables():
    j = np.arange(SEQ_DEVS)
    ang = 2 * np.pi * (j[:, None] + 0.25) * j[None, :] / SEQ_DEVS
    eye = np.eye(OWN)
    parts = []
    for part in (np.cos(ang), -np.sin(ang)):
        parts.append(np.einsum("jp,ab->ajpb", part, eye).reshape(CHANS, CHANS))
    first = np.concatenate(parts, 0)
    m = np.arange(BLOCK)
    ang = 2 * np.pi * ((m[:, None] * m[None, :]) % BLOCK) / BLOCK
    cos, sin = np.cos(ang), np.sin(ang)
    second = np.block([[cos, -sin], [sin, cos]])
    ang = 2 * np.pi * (j[:, None] + 0.25) * m[None, :] / TOTAL
    turn = np.stack([np.cos(ang), -np.sin(ang)])
    cast = lambda a: a.astype(np.float32).astype(ml_dtypes.bfloat16)
    return cast(first), cast(first.T), cast(second), turn.astype(np.float32)


def nt(a, b):
    return lax.dot_general(a, b, (((1,), (1,)), ((), ())), preferred_element_type=f32)


def kernel(
    gate_out_hbm, gate_in_hbm, values_hbm, grad_out_hbm, w_hbm, filt_hbm, skip_ref, first_hbm, last_hbm, second_hbm, turn_ref,
    RB, RS, done_hbm,
    G, W, first, last, second, gate_out, gate_in, values, filt,
    goT, SB, XB, SD, XD, OB, KS, acc, gz, RV, done, Y, Zs,
    lsem, dsem, ownsem, gsem, sx, rx, sf, rf, sz, rz, sa, ra, sd, rd, so, ro, sk, rk,
):
    s, c = lax.axis_index("seq"), lax.axis_index("ch")
    zbase = (c // 4) * 4
    x = lax.rem(c, 4)
    right, left, far = (s, zbase + lax.rem(x + 1, 4)), (s, zbase + lax.rem(x + 3, 4)), (s, lax.rem(c + 4, 8))

    def block(q, step):
        base = zbase if q == 0 else 4 - zbase
        return base + lax.rem(x + step + 4, 4)

    barrier = pltpu.get_barrier_semaphore()
    for dev in (right, left, far):
        pl.semaphore_signal(barrier, inc=1, device_id=dev, device_id_type=MESH)

    def greet(i, _):
        pl.semaphore_signal(barrier, inc=1, device_id=(lax.rem(s + i, SEQ_DEVS), c), device_id_type=MESH)
        return 0

    lax.fori_loop(1, SEQ_DEVS, greet, 0)
    loads = [(gate_in_hbm, gate_in), (values_hbm, values), (filt_hbm, filt), (gate_out_hbm, gate_out), (w_hbm, W),
             (first_hbm, first), (second_hbm, second), (last_hbm, last)]
    own = pltpu.make_async_copy(grad_out_hbm, G.at[c], gsem)
    own.start()
    loads = [pltpu.make_async_copy(a, b, lsem.at[i]) for i, (a, b) in enumerate(loads)]
    for cp in loads[:4]:
        cp.start()

    pl.semaphore_wait(barrier, SEQ_DEVS + 2)

    def remote(src, dst, ssem, rsem, dev):
        return pltpu.make_async_remote_copy(
            src_ref=src, dst_ref=dst, send_sem=ssem, recv_sem=rsem, device_id=dev, device_id_type=MESH
        )

    def xcopy(q, d, k, step=0):
        ref = G.at[block(q, step), pl.ds(k * CR, CR)]
        return remote(ref, ref, sx.at[q, d, k], rx.at[q, d, k], (right, left)[d])

    def fcopy(q, d, k, step):
        ref = G.at[block(q, step), pl.ds(k * CR, CR)]
        return remote(ref, ref, sf.at[q, d, k // 2], rf.at[q, d, k // 2], (right, left)[d])

    def zcopy(k, q=0):
        ref = G.at[block(q, 0), pl.ds(k * CR, CR)]
        return remote(ref, ref, sz.at[k], rz.at[k], far)

    def spread_start(buf, dst, ssem, rsem, first=1, end=SEQ_DEVS):
        def one(i, _):
            d = lax.rem(s + i, SEQ_DEVS)
            remote(buf.at[d], dst.at[s], ssem, rsem, (d, c)).start()
            return 0

        lax.fori_loop(first, end, one, 0)

    def spread_wait(buf, sem):
        part = buf.at[pl.ds(0, SEQ_DEVS - 1)]
        pltpu.make_async_copy(part, part, sem).wait()

    even, odd = tuple(range(0, CHUNKS, 2)), tuple(range(1, CHUNKS, 2))
    own.wait()
    for a, b in zip(even, odd):
        xcopy(0, 0, a).start()
        xcopy(0, 1, b).start()
    for k in range(CHUNKS):
        zcopy(k).start()
    for cp in loads[4:]:
        cp.start()

    def stage(f, columns):
        SB[f] = columns.T.astype(bf16).reshape(SEQ_DEVS, OWN, BLOCK)
        XB[f, pl.ds(s, 1)] = SB[f, pl.ds(s, 1)]

    def send_field(f, part, parts):
        size = SEQ_DEVS // parts
        spread_start(SB.at[f], XB.at[f], sa.at[f], ra.at[f], max(part * size, 1), (part + 1) * size)

    for i in range(5):
        loads[i].wait()
    gated = (gate_in[...].astype(f32) * values[...].astype(f32)).astype(bf16)
    goT[...] = gate_out[...].astype(f32).T

    def multiply(q, step, begin=False):
        h = block(q, step)
        cols = pl.ds(pl.multiple_of(h * WIDTH, WIDTH), WIDTH)
        part = nt(W[:, cols], G[h])
        acc[...] = part if begin else acc[...] + part

    def multiply_half(step, half):
        h = block(1, step)
        cols = pl.ds(pl.multiple_of(h * WIDTH, WIDTH), WIDTH)
        rows = slice(half * HALF, (half + 1) * HALF)
        acc[:, rows] += nt(W[:, cols], G[h, rows])

    def half_done(half):
        lo = half * CHUNKS // 2
        ks = range(lo, lo + CHUNKS // 2)
        multiply_half(0, half)
        for d in range(2):
            got(1, d, [k for k in ks if k % 2 != d])
            multiply_half((-1, 1)[d], half)
        for k in ks:
            fcopy(1, k % 2, k, 2).wait_recv()
        multiply_half(2, half)

    def send_half(half):
        rows = slice(half * HALF, (half + 1) * HALF)
        SD[half] = (acc[:, rows] * goT[:, rows]).astype(bf16).reshape(SEQ_DEVS, OWN, HALF)
        spread_start(SD.at[half], XD.at[half], sd.at[half], rd.at[half])
        XD[half, pl.ds(s, 1)] = SD[half, pl.ds(s, 1)]

    def got(q, d, ks):
        for k in ks:
            xcopy(q, d, k, (-1, 1)[d]).wait_recv()

    def pass_on(q, d, k):
        got(q, d, (k,))
        fcopy(q, d, k, (-1, 1)[d]).start()

    def z_step(k):
        if k < CHUNKS:
            zcopy(k, 1).wait_recv()
            xcopy(1, k % 2, k).start()
        if 0 <= k - DEFER < CHUNKS:
            xcopy(1, 1 - k % 2, k - DEFER).start()

    def finish_side(q, d):
        got(q, d, (odd, even)[d])
        multiply(q, (-1, 1)[d])

    def finish_far(q):
        for k in even:
            fcopy(q, 0, k, 2).wait_recv()
        for k in odd:
            fcopy(q, 1, k, 2).wait_recv()
        multiply(q, 2)

    groups = ROWS // SEQ_DEVS
    t_re, t_im = turn_ref[0][None], turn_ref[1][None]

    def fold(a):
        return a.reshape(groups, SEQ_DEVS, BLOCK)

    def both():
        return jnp.concatenate([XD[half].reshape(CHANS, HALF) for half in range(2)], axis=1)

    def forward(f):
        def one(i, _):
            rows = pl.ds(pl.multiple_of(i * ROWS, ROWS), ROWS)
            rows_im = pl.ds(pl.multiple_of(CHANS + i * ROWS, ROWS), ROWS)
            data = XB[f].reshape(CHANS, BLOCK) if f < 2 else both()
            re = fold(jnp.dot(first[rows, :], data, preferred_element_type=f32))
            im = fold(jnp.dot(first[rows_im, :], data, preferred_element_type=f32))
            z_re = (re * t_re - im * t_im).astype(bf16).reshape(ROWS, BLOCK)
            z_im = (re * t_im + im * t_re).astype(bf16).reshape(ROWS, BLOCK)
            Y[f, rows, :] = jnp.dot(
                z_re, second[:BLOCK, :], preferred_element_type=f32
            ) + jnp.dot(z_im, second[BLOCK:, :], preferred_element_type=f32)
            return 0

        lax.fori_loop(0, CHANS // ROWS, one, 0)

    def inverse(f, a, b):
        sign = 1.0 if f == 0 else -1.0

        def one(i, _):
            rows = pl.ds(pl.multiple_of(i * ROWS, ROWS), ROWS)
            rows_im = pl.ds(pl.multiple_of(CHANS + i * ROWS, ROWS), ROWS)
            a_re, a_im = Y[a, rows, :BLOCK], Y[a, rows, BLOCK:] * sign
            b_re, b_im = Y[b, rows, :BLOCK], Y[b, rows, BLOCK:]
            p_re = (a_re * b_re - a_im * b_im).astype(bf16)
            p_im = (a_re * b_im + a_im * b_re).astype(bf16)
            v = nt(p_re, second[:, :BLOCK]) + nt(p_im, second[:, BLOCK:])
            re, im = fold(v[:, :BLOCK]), fold(v[:, BLOCK:])
            Zs[rows, :] = (re * t_re + im * t_im).astype(bf16).reshape(ROWS, BLOCK)
            Zs[rows_im, :] = (im * t_re - re * t_im).astype(bf16).reshape(ROWS, BLOCK)
            return 0

        lax.fori_loop(0, CHANS // ROWS, one, 0)

        def two(i, _):
            rows = pl.ds(pl.multiple_of(i * ROWS, ROWS), ROWS)
            out = jnp.dot(last[rows, :], Zs[...], preferred_element_type=f32) * SCALE
            OB[f, pl.ds(i * (ROWS // OWN), ROWS // OWN)] = out.astype(bf16).reshape(ROWS // OWN, OWN, BLOCK)
            return 0

        lax.fori_loop(0, CHANS // ROWS, two, 0)
        dst = RB if f == 2 else RV.at[f]
        spread_start(OB.at[f], dst, so.at[f], ro.at[f])
        pltpu.make_async_copy(OB.at[f, s], dst.at[s], ownsem.at[f]).start()

    stage(1, filt[...].astype(f32))
    send_field(1, 0, 4)
    multiply(0, 0, begin=True)
    pass_on(0, 0, 0)
    pass_on(0, 1, 1)
    xcopy(0, 0, 1).start()
    xcopy(0, 1, 0).start()
    z_step(0)
    send_field(1, 1, 4)
    stage(0, gated.astype(f32))
    pass_on(0, 0, 2)
    pass_on(0, 1, 3)
    xcopy(0, 0, 3).start()
    xcopy(0, 1, 2).start()
    send_field(1, 2, 4)
    z_step(1)
    finish_side(0, 0)
    send_field(1, 3, 4)
    finish_side(0, 1)
    z_step(2)
    send_field(0, 0, 4)
    pass_on(1, 0, 0)
    pass_on(1, 1, 1)
    send_field(0, 1, 4)
    finish_far(0)
    z_step(3)
    send_field(0, 2, 4)
    half_done(0)
    send_field(0, 3, 4)
    pass_on(1, 0, 2)
    pass_on(1, 1, 3)
    send_half(0)
    half_done(1)
    send_half(1)
    for i in range(5, 8):
        loads[i].wait()
    spread_wait(XB.at[1], ra.at[1])
    forward(1)
    spread_wait(XB.at[0], ra.at[0])
    forward(0)
    inverse(0, 1, 0)


    for half in range(2):
        spread_wait(XD.at[half], rd.at[half])
    forward(2)
    inverse(1, 1, 2)
    total = jnp.sum(XB[0].astype(f32) * both().reshape(XB.shape[1:]).astype(f32), axis=0)
    total = jnp.sum(total, axis=1, keepdims=True) * (1.0 / TOTAL)
    here = lax.rem(lax.broadcasted_iota(jnp.int32, (OWN, 128), 1), OWN) == lax.broadcasted_iota(jnp.int32, (OWN, 128), 0)
    KS[...] = jnp.sum(jnp.where(here, total, 0.0), axis=0, keepdims=True)
    pltpu.make_async_copy(KS, RS.at[s], ownsem.at[3]).start()

    def tell(i, _):
        d = lax.rem(s + i, SEQ_DEVS)
        remote(KS, RS.at[s], sk, rk, (d, c)).start()
        return 0

    lax.fori_loop(1, SEQ_DEVS, tell, 0)

    inverse(2, 0, 2)
    gz[...] = acc[...].T


    def back(f):
        spread_wait(RV.at[f], ro.at[f])
        pltpu.make_async_copy(OB.at[f, s], RV.at[f, s], ownsem.at[f]).wait()
        return RV[f].reshape(CHANS, BLOCK).astype(f32).T

    skip = skip_ref[...]
    gated = (gate_in[...].astype(f32) * values[...].astype(f32)).astype(bf16).astype(f32)
    done[0] = (gz[...] * (back(0) + skip * gated)).astype(bf16)
    put = [pltpu.make_async_copy(done.at[i], done_hbm.at[i], dsem.at[i]) for i in range(3)]
    put[0].start()
    grad_y = (gz[...] * gate_out[...].astype(f32)).astype(bf16).astype(f32)
    mixed = back(1) + skip * grad_y
    done[1] = (mixed * values[...].astype(f32)).astype(bf16)
    done[2] = (mixed * gate_in[...].astype(f32)).astype(bf16)
    put[1].start()
    put[2].start()
    spread_wait(RB, ro.at[2])
    pltpu.make_async_copy(OB.at[2, s], RB.at[s], ownsem.at[2]).wait()
    for cp in put:
        cp.wait()
    spread_wait(RS, rk)
    pltpu.make_async_copy(KS, RS.at[s], ownsem.at[3]).wait()

    for q in range(2):
        for d in range(2):
            for k in range(CHUNKS):
                xcopy(q, d, k).wait_send()
            for k in (even, odd)[d]:
                fcopy(q, d, k, (-1, 1)[d]).wait_send()
    for k in range(CHUNKS):
        zcopy(k).wait_send()
    for f in range(2):
        spread_wait(SB.at[f], sa.at[f])
        spread_wait(SD.at[f], sd.at[f])
    for f in range(3):
        spread_wait(OB.at[f], so.at[f])
    spread_wait(RS, sk)


def finish(back_ref, sums_ref, done_ref, ggo_ref, ggi_ref, gv_ref, gf_ref, gs_ref):
    gf_ref[...] = back_ref[...].reshape(-1, BLOCK).astype(f32).T.astype(bf16)
    ggo_ref[...] = done_ref[0]
    ggi_ref[...] = done_ref[1]
    gv_ref[...] = done_ref[2]

    @pl.when(pl.program_id(0) == 0)
    def _():
        sums = jnp.concatenate([sums_ref[:, 0, :]] * (CHANS // 128), axis=1)
        device = lax.broadcasted_iota(jnp.int32, sums.shape, 1) // OWN
        keep = device == lax.broadcasted_iota(jnp.int32, sums.shape, 0)
        gs_ref[...] = jnp.sum(jnp.where(keep, sums, 0.0), axis=0).astype(bf16)


def body(gate_out, gate_in, values, grad_out, w_out, filter_raw, skip):
    first, last, second, turn = tables()
    anyspace = pl.BlockSpec(memory_space=pl.ANY)
    hbm = pl.BlockSpec(memory_space=pltpu.HBM)
    vmem = pl.BlockSpec(memory_space=pltpu.VMEM)
    dma = pltpu.SemaphoreType.DMA
    field = (3, SEQ_DEVS, OWN, BLOCK)
    local = (BLOCK, CHANS)
    back, sums, done = pl.pallas_call(
        kernel,
        out_shape=(
            jax.ShapeDtypeStruct(field[1:], bf16),
            jax.ShapeDtypeStruct((SEQ_DEVS, 1, 128), f32),
            jax.ShapeDtypeStruct((3,) + local, bf16),
        ),
        in_specs=[hbm] * 6 + [vmem] + [anyspace] * 3 + [vmem],
        out_specs=(hbm,) * 3,
        scratch_shapes=[
            pltpu.VMEM((CH_DEVS, BLOCK, WIDTH), bf16),
            pltpu.VMEM((CHANS, CH_DEVS * WIDTH), bf16),
            pltpu.VMEM((2 * CHANS, CHANS), bf16),
            pltpu.VMEM((CHANS, 2 * CHANS), bf16),
            pltpu.VMEM((2 * BLOCK, 2 * BLOCK), bf16),
            pltpu.VMEM(local, bf16),
            pltpu.VMEM(local, bf16),
            pltpu.VMEM(local, bf16),
            pltpu.VMEM(local, bf16),
            pltpu.VMEM((CHANS, BLOCK), f32),
            pltpu.VMEM((2,) + field[1:], bf16),
            pltpu.VMEM((2,) + field[1:], bf16),
            pltpu.VMEM((2, SEQ_DEVS, OWN, HALF), bf16),
            pltpu.VMEM((2, SEQ_DEVS, OWN, HALF), bf16),
            pltpu.VMEM(field, bf16),
            pltpu.VMEM((1, 128), f32),
            pltpu.VMEM((CHANS, BLOCK), f32),
            pltpu.VMEM(local, f32),
            pltpu.VMEM((2,) + field[1:], bf16),
            pltpu.VMEM((3,) + local, bf16),
            pltpu.VMEM((3, CHANS, 2 * BLOCK), f32),
            pltpu.VMEM((2 * CHANS, BLOCK), bf16),
            dma((8,)),
            dma((3,)),
            dma((4,)),
            dma,
            dma((2, 2, CHUNKS)),
            dma((2, 2, CHUNKS)),
            dma((2, 2, CHUNKS // 2)),
            dma((2, 2, CHUNKS // 2)),
            dma((CHUNKS,)),
            dma((CHUNKS,)),
            dma((2,)),
            dma((2,)),
            dma((2,)),
            dma((2,)),
            dma((3,)),
            dma((3,)),
            dma,
            dma,
        ],
        compiler_params=pltpu.CompilerParams(collective_id=0, has_side_effects=True, vmem_limit_bytes=60 << 20),
        name="transforms",
    )(gate_out, gate_in, values, grad_out, w_out, filter_raw, skip[None, :], first, last, second, turn)
    out = jax.ShapeDtypeStruct(local, bf16)
    cols = CHANS // STEPS
    tile = pl.BlockSpec((BLOCK, cols), lambda i: (0, i))
    outs = pl.pallas_call(
        finish,
        grid=(STEPS,),
        out_shape=(out, out, out, out, jax.ShapeDtypeStruct((CHANS,), bf16)),
        in_specs=[
            pl.BlockSpec((SEQ_DEVS // STEPS, OWN, BLOCK), lambda i: (i, 0, 0)),
            pl.BlockSpec((SEQ_DEVS, 1, 128), lambda i: (0, 0, 0)),
            pl.BlockSpec((3, BLOCK, cols), lambda i: (0, 0, i)),
        ],
        out_specs=(tile, tile, tile, tile, pl.BlockSpec((CHANS,), lambda i: (0,))),
        compiler_params=pltpu.CompilerParams(vmem_limit_bytes=60 << 20),
        name="gradients",
    )(back, sums, done)
    return outs


def solution(mesh):
    return jax.shard_map(
        body,
        mesh=mesh,
        in_specs=(
            P("seq", "ch"),
            P("seq", "ch"),
            P("seq", "ch"),
            P("seq", "ch"),
            P("ch", None),
            P("seq", "ch"),
            P("ch"),
        ),
        out_specs=(P("seq", "ch"), P("seq", "ch"), P("seq", "ch"), P("seq", "ch"), P("ch")),
        check_vma=False,
    )
```

```python
import functools
import math

import jax
import jax.numpy as jnp
import ml_dtypes
import numpy as np
from jax import lax
from jax.experimental import pallas as pl
from jax.experimental.pallas import tpu as pltpu
from jax.sharding import PartitionSpec as P

MESH = pl.DeviceIdType.MESH
bf16, f32 = jnp.bfloat16, jnp.float32

SEQ_DEVS = 32
CH_DEVS = 8
BLOCK = 256
CHANS = 512
OWN = CHANS // SEQ_DEVS
TOTAL = SEQ_DEVS * BLOCK
WIDTH = 1024
CHUNKS = 4
CR = BLOCK // CHUNKS
HALF = BLOCK // 2
STEPS = 2
ROWS = 256
DEFER = 0
SCALE = 1.0 / (TOTAL * math.sqrt(TOTAL))


def tables():
    j = np.arange(SEQ_DEVS)
    ang = 2 * np.pi * (j[:, None] + 0.25) * j[None, :] / SEQ_DEVS
    eye = np.eye(OWN)
    parts = []
    for part in (np.cos(ang), -np.sin(ang)):
        parts.append(np.einsum("jp,ab->ajpb", part, eye).reshape(CHANS, CHANS))
    first = np.concatenate(parts, 0)
    m = np.arange(BLOCK)
    ang = 2 * np.pi * ((m[:, None] * m[None, :]) % BLOCK) / BLOCK
    cos, sin = np.cos(ang), np.sin(ang)
    second = np.block([[cos, -sin], [sin, cos]])
    ang = 2 * np.pi * (j[:, None] + 0.25) * m[None, :] / TOTAL
    turn = np.stack([np.cos(ang), -np.sin(ang)])
    cast = lambda a: a.astype(np.float32).astype(ml_dtypes.bfloat16)
    return cast(first), cast(first.T), cast(second), turn.astype(np.float32)


def nt(a, b):
    return lax.dot_general(a, b, (((1,), (1,)), ((), ())), preferred_element_type=f32)


def kernel(
    gate_out_hbm, gate_in_hbm, values_hbm, grad_out_hbm, w_hbm, filt_hbm, skip_ref, first_hbm, last_hbm, second_hbm, turn_ref,
    RB, RS, done_hbm,
    G, W, first, last, second, gate_out, gate_in, values, filt,
    goT, SB, XB, SD, XD, OB, KS, acc, gz, RV, done, Y, Zs,
    lsem, dsem, ownsem, gsem, sx, rx, sf, rf, sz, rz, sa, ra, sd, rd, so, ro, sk, rk,
):
    s, c = lax.axis_index("seq"), lax.axis_index("ch")
    zbase = (c // 4) * 4
    x = lax.rem(c, 4)
    right, left, far = (s, zbase + lax.rem(x + 1, 4)), (s, zbase + lax.rem(x + 3, 4)), (s, lax.rem(c + 4, 8))

    def block(q, step):
        base = zbase if q == 0 else 4 - zbase
        return base + lax.rem(x + step + 4, 4)

    barrier = pltpu.get_barrier_semaphore()
    for dev in (right, left, far):
        pl.semaphore_signal(barrier, inc=1, device_id=dev, device_id_type=MESH)

    def greet(i, _):
        pl.semaphore_signal(barrier, inc=1, device_id=(lax.rem(s + i, SEQ_DEVS), c), device_id_type=MESH)
        return 0

    lax.fori_loop(1, SEQ_DEVS, greet, 0)
    loads = [(gate_in_hbm, gate_in), (values_hbm, values), (filt_hbm, filt), (gate_out_hbm, gate_out), (w_hbm, W),
             (first_hbm, first), (second_hbm, second), (last_hbm, last)]
    own = pltpu.make_async_copy(grad_out_hbm, G.at[c], gsem)
    own.start()
    loads = [pltpu.make_async_copy(a, b, lsem.at[i]) for i, (a, b) in enumerate(loads)]
    for cp in loads[:4]:
        cp.start()

    pl.semaphore_wait(barrier, SEQ_DEVS + 2)

    def remote(src, dst, ssem, rsem, dev):
        return pltpu.make_async_remote_copy(
            src_ref=src, dst_ref=dst, send_sem=ssem, recv_sem=rsem, device_id=dev, device_id_type=MESH
        )

    def xcopy(q, d, k, step=0):
        ref = G.at[block(q, step), pl.ds(k * CR, CR)]
        return remote(ref, ref, sx.at[q, d, k], rx.at[q, d, k], (right, left)[d])

    def fcopy(q, d, k, step):
        ref = G.at[block(q, step), pl.ds(k * CR, CR)]
        return remote(ref, ref, sf.at[q, d, k // 2], rf.at[q, d, k // 2], (right, left)[d])

    def zcopy(k, q=0):
        ref = G.at[block(q, 0), pl.ds(k * CR, CR)]
        return remote(ref, ref, sz.at[k], rz.at[k], far)

    def spread_start(buf, dst, ssem, rsem, first=1, end=SEQ_DEVS):
        def one(i, _):
            d = lax.rem(s + i, SEQ_DEVS)
            remote(buf.at[d], dst.at[s], ssem, rsem, (d, c)).start()
            return 0

        lax.fori_loop(first, end, one, 0)

    def spread_wait(buf, sem):
        part = buf.at[pl.ds(0, SEQ_DEVS - 1)]
        pltpu.make_async_copy(part, part, sem).wait()

    even, odd = tuple(range(0, CHUNKS, 2)), tuple(range(1, CHUNKS, 2))
    own.wait()
    for a, b in zip(even, odd):
        xcopy(0, 0, a).start()
        xcopy(0, 1, b).start()
    for k in range(CHUNKS):
        zcopy(k).start()
    for cp in loads[4:]:
        cp.start()

    def stage(f, columns):
        SB[f] = columns.T.astype(bf16).reshape(SEQ_DEVS, OWN, BLOCK)
        XB[f, pl.ds(s, 1)] = SB[f, pl.ds(s, 1)]

    def send_field(f, part, parts):
        size = SEQ_DEVS // parts
        spread_start(SB.at[f], XB.at[f], sa.at[f], ra.at[f], max(part * size, 1), (part + 1) * size)

    for i in range(5):
        loads[i].wait()
    gated = (gate_in[...].astype(f32) * values[...].astype(f32)).astype(bf16)
    goT[...] = gate_out[...].astype(f32).T

    def multiply(q, step, begin=False):
        h = block(q, step)
        cols = pl.ds(pl.multiple_of(h * WIDTH, WIDTH), WIDTH)
        part = nt(W[:, cols], G[h])
        acc[...] = part if begin else acc[...] + part

    def multiply_half(step, half):
        h = block(1, step)
        cols = pl.ds(pl.multiple_of(h * WIDTH, WIDTH), WIDTH)
        rows = slice(half * HALF, (half + 1) * HALF)
        acc[:, rows] += nt(W[:, cols], G[h, rows])

    def half_done(half):
        lo = half * CHUNKS // 2
        ks = range(lo, lo + CHUNKS // 2)
        multiply_half(0, half)
        for d in range(2):
            got(1, d, [k for k in ks if k % 2 != d])
            multiply_half((-1, 1)[d], half)
        for k in ks:
            fcopy(1, k % 2, k, 2).wait_recv()
        multiply_half(2, half)

    def send_half(half):
        rows = slice(half * HALF, (half + 1) * HALF)
        SD[half] = (acc[:, rows] * goT[:, rows]).astype(bf16).reshape(SEQ_DEVS, OWN, HALF)
        spread_start(SD.at[half], XD.at[half], sd.at[half], rd.at[half])
        XD[half, pl.ds(s, 1)] = SD[half, pl.ds(s, 1)]

    def got(q, d, ks):
        for k in ks:
            xcopy(q, d, k, (-1, 1)[d]).wait_recv()

    def pass_on(q, d, k):
        got(q, d, (k,))
        fcopy(q, d, k, (-1, 1)[d]).start()

    def z_step(k):
        if k < CHUNKS:
            zcopy(k, 1).wait_recv()
            xcopy(1, k % 2, k).start()
        if 0 <= k - DEFER < CHUNKS:
            xcopy(1, 1 - k % 2, k - DEFER).start()

    def finish_side(q, d):
        got(q, d, (odd, even)[d])
        multiply(q, (-1, 1)[d])

    def finish_far(q):
        for k in even:
            fcopy(q, 0, k, 2).wait_recv()
        for k in odd:
            fcopy(q, 1, k, 2).wait_recv()
        multiply(q, 2)

    groups = ROWS // SEQ_DEVS
    t_re, t_im = turn_ref[0][None], turn_ref[1][None]

    def fold(a):
        return a.reshape(groups, SEQ_DEVS, BLOCK)

    def both():
        return jnp.concatenate([XD[half].reshape(CHANS, HALF) for half in range(2)], axis=1)

    def forward(f):
        def one(i, _):
            rows = pl.ds(pl.multiple_of(i * ROWS, ROWS), ROWS)
            rows_im = pl.ds(pl.multiple_of(CHANS + i * ROWS, ROWS), ROWS)
            data = XB[f].reshape(CHANS, BLOCK) if f < 2 else both()
            re = fold(jnp.dot(first[rows, :], data, preferred_element_type=f32))
            im = fold(jnp.dot(first[rows_im, :], data, preferred_element_type=f32))
            z_re = (re * t_re - im * t_im).astype(bf16).reshape(ROWS, BLOCK)
            z_im = (re * t_im + im * t_re).astype(bf16).reshape(ROWS, BLOCK)
            Y[f, rows, :] = jnp.dot(
                z_re, second[:BLOCK, :], preferred_element_type=f32
            ) + jnp.dot(z_im, second[BLOCK:, :], preferred_element_type=f32)
            return 0

        lax.fori_loop(0, CHANS // ROWS, one, 0)

    def inverse(f, a, b):
        sign = 1.0 if f == 0 else -1.0

        def one(i, _):
            rows = pl.ds(pl.multiple_of(i * ROWS, ROWS), ROWS)
            rows_im = pl.ds(pl.multiple_of(CHANS + i * ROWS, ROWS), ROWS)
            a_re, a_im = Y[a, rows, :BLOCK], Y[a, rows, BLOCK:] * sign
            b_re, b_im = Y[b, rows, :BLOCK], Y[b, rows, BLOCK:]
            p_re = (a_re * b_re - a_im * b_im).astype(bf16)
            p_im = (a_re * b_im + a_im * b_re).astype(bf16)
            v = nt(p_re, second[:, :BLOCK]) + nt(p_im, second[:, BLOCK:])
            re, im = fold(v[:, :BLOCK]), fold(v[:, BLOCK:])
            Zs[rows, :] = (re * t_re + im * t_im).astype(bf16).reshape(ROWS, BLOCK)
            Zs[rows_im, :] = (im * t_re - re * t_im).astype(bf16).reshape(ROWS, BLOCK)
            return 0

        lax.fori_loop(0, CHANS // ROWS, one, 0)

        def two(i, _):
            rows = pl.ds(pl.multiple_of(i * ROWS, ROWS), ROWS)
            out = jnp.dot(last[rows, :], Zs[...], preferred_element_type=f32) * SCALE
            OB[f, pl.ds(i * (ROWS // OWN), ROWS // OWN)] = out.astype(bf16).reshape(ROWS // OWN, OWN, BLOCK)
            return 0

        lax.fori_loop(0, CHANS // ROWS, two, 0)
        dst = RB if f == 2 else RV.at[f]
        spread_start(OB.at[f], dst, so.at[f], ro.at[f])
        pltpu.make_async_copy(OB.at[f, s], dst.at[s], ownsem.at[f]).start()

    stage(1, filt[...].astype(f32))
    send_field(1, 0, 4)
    multiply(0, 0, begin=True)
    pass_on(0, 0, 0)
    pass_on(0, 1, 1)
    xcopy(0, 0, 1).start()
    xcopy(0, 1, 0).start()
    z_step(0)
    send_field(1, 1, 4)
    stage(0, gated.astype(f32))
    pass_on(0, 0, 2)
    pass_on(0, 1, 3)
    xcopy(0, 0, 3).start()
    xcopy(0, 1, 2).start()
    send_field(1, 2, 4)
    z_step(1)
    finish_side(0, 0)
    send_field(1, 3, 4)
    finish_side(0, 1)
    z_step(2)
    send_field(0, 0, 4)
    pass_on(1, 0, 0)
    pass_on(1, 1, 1)
    send_field(0, 1, 4)
    z_step(3)
    finish_far(0)
    send_field(0, 2, 4)
    half_done(0)
    send_field(0, 3, 4)
    pass_on(1, 0, 2)
    pass_on(1, 1, 3)
    send_half(0)
    half_done(1)
    send_half(1)
    for i in range(5, 8):
        loads[i].wait()
    spread_wait(XB.at[1], ra.at[1])
    forward(1)
    spread_wait(XB.at[0], ra.at[0])
    forward(0)
    inverse(0, 1, 0)


    for half in range(2):
        spread_wait(XD.at[half], rd.at[half])
    forward(2)
    inverse(1, 1, 2)
    total = jnp.sum(XB[0].astype(f32) * both().reshape(XB.shape[1:]).astype(f32), axis=0)
    total = jnp.sum(total, axis=1, keepdims=True) * (1.0 / TOTAL)
    here = lax.rem(lax.broadcasted_iota(jnp.int32, (OWN, 128), 1), OWN) == lax.broadcasted_iota(jnp.int32, (OWN, 128), 0)
    KS[...] = jnp.sum(jnp.where(here, total, 0.0), axis=0, keepdims=True)
    pltpu.make_async_copy(KS, RS.at[s], ownsem.at[3]).start()

    def tell(i, _):
        d = lax.rem(s + i, SEQ_DEVS)
        remote(KS, RS.at[s], sk, rk, (d, c)).start()
        return 0

    lax.fori_loop(1, SEQ_DEVS, tell, 0)

    inverse(2, 0, 2)
    gz[...] = acc[...].T


    def back(f):
        spread_wait(RV.at[f], ro.at[f])
        pltpu.make_async_copy(OB.at[f, s], RV.at[f, s], ownsem.at[f]).wait()
        return RV[f].reshape(CHANS, BLOCK).astype(f32).T

    skip = skip_ref[...]
    gated = (gate_in[...].astype(f32) * values[...].astype(f32)).astype(bf16).astype(f32)
    done[0] = (gz[...] * (back(0) + skip * gated)).astype(bf16)
    put = [pltpu.make_async_copy(done.at[i], done_hbm.at[i], dsem.at[i]) for i in range(3)]
    put[0].start()
    grad_y = (gz[...] * gate_out[...].astype(f32)).astype(bf16).astype(f32)
    mixed = back(1) + skip * grad_y
    done[1] = (mixed * values[...].astype(f32)).astype(bf16)
    done[2] = (mixed * gate_in[...].astype(f32)).astype(bf16)
    put[1].start()
    put[2].start()
    spread_wait(RB, ro.at[2])
    pltpu.make_async_copy(OB.at[2, s], RB.at[s], ownsem.at[2]).wait()
    for cp in put:
        cp.wait()
    spread_wait(RS, rk)
    pltpu.make_async_copy(KS, RS.at[s], ownsem.at[3]).wait()

    for q in range(2):
        for d in range(2):
            for k in range(CHUNKS):
                xcopy(q, d, k).wait_send()
            for k in (even, odd)[d]:
                fcopy(q, d, k, (-1, 1)[d]).wait_send()
    for k in range(CHUNKS):
        zcopy(k).wait_send()
    for f in range(2):
        spread_wait(SB.at[f], sa.at[f])
        spread_wait(SD.at[f], sd.at[f])
    for f in range(3):
        spread_wait(OB.at[f], so.at[f])
    spread_wait(RS, sk)


def finish(back_ref, sums_ref, done_ref, ggo_ref, ggi_ref, gv_ref, gf_ref, gs_ref):
    gf_ref[...] = back_ref[...].reshape(-1, BLOCK).astype(f32).T.astype(bf16)
    ggo_ref[...] = done_ref[0]
    ggi_ref[...] = done_ref[1]
    gv_ref[...] = done_ref[2]

    @pl.when(pl.program_id(0) == 0)
    def _():
        sums = jnp.concatenate([sums_ref[:, 0, :]] * (CHANS // 128), axis=1)
        device = lax.broadcasted_iota(jnp.int32, sums.shape, 1) // OWN
        keep = device == lax.broadcasted_iota(jnp.int32, sums.shape, 0)
        gs_ref[...] = jnp.sum(jnp.where(keep, sums, 0.0), axis=0).astype(bf16)


def body(gate_out, gate_in, values, grad_out, w_out, filter_raw, skip):
    first, last, second, turn = tables()
    anyspace = pl.BlockSpec(memory_space=pl.ANY)
    hbm = pl.BlockSpec(memory_space=pltpu.HBM)
    vmem = pl.BlockSpec(memory_space=pltpu.VMEM)
    dma = pltpu.SemaphoreType.DMA
    field = (3, SEQ_DEVS, OWN, BLOCK)
    local = (BLOCK, CHANS)
    back, sums, done = pl.pallas_call(
        kernel,
        out_shape=(
            jax.ShapeDtypeStruct(field[1:], bf16),
            jax.ShapeDtypeStruct((SEQ_DEVS, 1, 128), f32),
            jax.ShapeDtypeStruct((3,) + local, bf16),
        ),
        in_specs=[hbm] * 6 + [vmem] + [anyspace] * 3 + [vmem],
        out_specs=(hbm,) * 3,
        scratch_shapes=[
            pltpu.VMEM((CH_DEVS, BLOCK, WIDTH), bf16),
            pltpu.VMEM((CHANS, CH_DEVS * WIDTH), bf16),
            pltpu.VMEM((2 * CHANS, CHANS), bf16),
            pltpu.VMEM((CHANS, 2 * CHANS), bf16),
            pltpu.VMEM((2 * BLOCK, 2 * BLOCK), bf16),
            pltpu.VMEM(local, bf16),
            pltpu.VMEM(local, bf16),
            pltpu.VMEM(local, bf16),
            pltpu.VMEM(local, bf16),
            pltpu.VMEM((CHANS, BLOCK), f32),
            pltpu.VMEM((2,) + field[1:], bf16),
            pltpu.VMEM((2,) + field[1:], bf16),
            pltpu.VMEM((2, SEQ_DEVS, OWN, HALF), bf16),
            pltpu.VMEM((2, SEQ_DEVS, OWN, HALF), bf16),
            pltpu.VMEM(field, bf16),
            pltpu.VMEM((1, 128), f32),
            pltpu.VMEM((CHANS, BLOCK), f32),
            pltpu.VMEM(local, f32),
            pltpu.VMEM((2,) + field[1:], bf16),
            pltpu.VMEM((3,) + local, bf16),
            pltpu.VMEM((3, CHANS, 2 * BLOCK), f32),
            pltpu.VMEM((2 * CHANS, BLOCK), bf16),
            dma((8,)),
            dma((3,)),
            dma((4,)),
            dma,
            dma((2, 2, CHUNKS)),
            dma((2, 2, CHUNKS)),
            dma((2, 2, CHUNKS // 2)),
            dma((2, 2, CHUNKS // 2)),
            dma((CHUNKS,)),
            dma((CHUNKS,)),
            dma((2,)),
            dma((2,)),
            dma((2,)),
            dma((2,)),
            dma((3,)),
            dma((3,)),
            dma,
            dma,
        ],
        compiler_params=pltpu.CompilerParams(collective_id=0, has_side_effects=True, vmem_limit_bytes=60 << 20),
        name="transforms",
    )(gate_out, gate_in, values, grad_out, w_out, filter_raw, skip[None, :], first, last, second, turn)
    out = jax.ShapeDtypeStruct(local, bf16)
    cols = CHANS // STEPS
    tile = pl.BlockSpec((BLOCK, cols), lambda i: (0, i))
    outs = pl.pallas_call(
        finish,
        grid=(STEPS,),
        out_shape=(out, out, out, out, jax.ShapeDtypeStruct((CHANS,), bf16)),
        in_specs=[
            pl.BlockSpec((SEQ_DEVS // STEPS, OWN, BLOCK), lambda i: (i, 0, 0)),
            pl.BlockSpec((SEQ_DEVS, 1, 128), lambda i: (0, 0, 0)),
            pl.BlockSpec((3, BLOCK, cols), lambda i: (0, 0, i)),
        ],
        out_specs=(tile, tile, tile, tile, pl.BlockSpec((CHANS,), lambda i: (0,))),
        compiler_params=pltpu.CompilerParams(vmem_limit_bytes=60 << 20),
        name="gradients",
    )(back, sums, done)
    return outs


def solution(mesh):
    return jax.shard_map(
        body,
        mesh=mesh,
        in_specs=(
            P("seq", "ch"),
            P("seq", "ch"),
            P("seq", "ch"),
            P("seq", "ch"),
            P("ch", None),
            P("seq", "ch"),
            P("ch"),
        ),
        out_specs=(P("seq", "ch"), P("seq", "ch"), P("seq", "ch"), P("seq", "ch"), P("ch")),
        check_vma=False,
    )
```
